1024 devices in a mesh: width: 16 (over z), hidden: 16 (over y, core), batch: 4 (over x).
Axes of the slice: x: 4, y: 8, z: 16, core: 2. Of those that a mesh axis runs over, the one named last changes fastest.
Arguments:
- tokens: bfloat16 [64, 2, 16384], P('batch', None, 'width'), may hold values from -40 to 40
- norm_gain: bfloat16 [16384], P('width'), may hold values from 0.5 to 1.5
- w_query: bfloat16 [16384, 16384], P('width', 'hidden'), may hold values from -0.046875 to 0.046875
- key_weight: bfloat16 [16384, 1024], P('width', 'hidden'), may hold values from -0.046875 to 0.046875
- value_weight: bfloat16 [16384, 1024], P('width', 'hidden'), may hold values from -0.046875 to 0.046875
- output_weight: bfloat16 [16384, 16384], P('hidden', 'width'), may hold values from -0.5 to 0.5
- rotated_key_cache: bfloat16 [64, 1024, 1024], P(('batch', 'hidden'), 'width'), may hold values from -64 to 64
- stored_value_cache: bfloat16 [64, 1024, 1024], P(('batch', 'hidden'), 'width'), may hold values from -6 to 6
- lengths: int32 [64], P(('batch', 'hidden')), may hold values from 2 to 1024, as said below
- positions: int32 [64], P(('batch', 'hidden')), may hold values from 0 to 4095
Outputs:
- layer_out: bfloat16 [64, 2, 16384], P(('batch', 'hidden'), None, 'width')
The draws below stay inside these ranges and needn't reach their ends.
Inputs may be any that keep to these rules, and one draw needn't show every extreme that they name: `lengths`: each row's number of valid cache entries; some row has exactly 1024.
All inputs are finite; a program needn't handle non-finite values.
Results may differ from the reference program's by a relative error of at most 0.011.
Values may be sent and summed in bfloat16 or wider, within the bound.
A program may use at most 64 MiB of HBM per device.

```python
import math
import jax
import jax.numpy as jnp
from jax import lax

MODEL_DIMENSION = 16384
QUERY_HEADS = 128
KEY_VALUE_HEADS = 8
HEAD_SIZE = 128
CONTEXT_PER_SLICE = 64
STEPS = 2
TOTAL_ROWS = 64
CACHE_CAPACITY = 1024
N_WIDTH = 16


def draw_tokens(key, part):
    key = jax.random.fold_in(key, 11)
    noise_seed, column_key, row_key = jax.random.split(key, 3)
    noise = jax.random.normal(noise_seed, (TOTAL_ROWS, STEPS, MODEL_DIMENSION), jnp.float32)
    column_scale = jnp.exp(jnp.linspace(math.log(0.35), math.log(1.05), MODEL_DIMENSION) + jax.random.uniform(column_key, (MODEL_DIMENSION,), jnp.float32) * math.log(3.0))
    row_scale = 0.3 * jnp.exp(jax.random.uniform(row_key, (TOTAL_ROWS, STEPS, 1), jnp.float32) * math.log(10.0))
    return jnp.clip(noise * column_scale * row_scale, -40.0, 40.0).astype(jnp.bfloat16)


def draw_rotated_key_cache(key, part):
    key = jax.random.fold_in(key, 23)
    noise_seed = jax.random.fold_in(key, 0)
    cache_state = jnp.clip(jax.random.normal(noise_seed, (TOTAL_ROWS, CACHE_CAPACITY, KEY_VALUE_HEADS * HEAD_SIZE), jnp.float32), -6.0, 6.0)
    return cache_state.astype(jnp.bfloat16)


def draw_lengths(key, part):
    key = jax.random.fold_in(key, 37)
    length_key, row_key = jax.random.split(key, 2)
    row_lengths = jax.random.randint(length_key, (TOTAL_ROWS,), 2, CACHE_CAPACITY + 1)
    longest = jax.random.randint(row_key, (), 0, TOTAL_ROWS)
    return row_lengths.at[longest].set(CACHE_CAPACITY)


def with_ends(entries, stream_key, least, high):
    extent = entries.shape
    place = [jax.random.randint(jax.random.fold_in(stream_key, axis), (), 0, extent[axis]) for axis in range(len(extent))]
    entries = entries.at[tuple(place)].set(least)
    longest = extent.index(max(extent))
    place[longest] = (place[longest] + 1) % extent[longest]
    return entries.at[tuple(place)].set(high)


def shard_levels(rng, shape, cuts, smallest, top_value):
    def one(axis_at, blocks):
        steps = jax.random.uniform(jax.random.fold_in(jax.random.fold_in(rng, 6), axis_at), (blocks,), jnp.float32, smallest / len(cuts), top_value / len(cuts))
        return jnp.repeat(jnp.exp(steps), shape[axis_at] // blocks).reshape((-1,) + (1,) * (len(shape) - axis_at - 1))

    loudness = one(*cuts[0])
    for cut in cuts[1:]:
        loudness = loudness * one(*cut)
    return loudness


def normal_values(rng, dims, scale, bound, cuts=(), kind=jnp.bfloat16):
    entries = jax.random.normal(rng, dims, jnp.float32) * scale
    if len(cuts) > 0:
        entries = shard_levels(rng, dims, cuts, -0.22, 0.18) * entries
    return jnp.clip(entries, min=-bound, max=bound).astype(kind)


def setup_inputs(seed: int = 0) -> dict:
    streams_of = jax.random.split(jax.random.key(seed), 11)
    tokens = draw_tokens(jax.random.fold_in(streams_of[10], 71), 0)
    norm_gain = jnp.clip(1.0 + 0.1 * jax.random.normal(streams_of[1], (MODEL_DIMENSION,), jnp.float32), 0.5, 1.5).astype(jnp.bfloat16)
    w_query = normal_values(streams_of[2], (MODEL_DIMENSION, QUERY_HEADS * HEAD_SIZE), MODEL_DIMENSION ** -0.5, 0.046875, ((0, 16), (1, 16)))
    key_weight = normal_values(streams_of[3], (MODEL_DIMENSION, KEY_VALUE_HEADS * HEAD_SIZE), MODEL_DIMENSION ** -0.5, 0.046875, ((0, 16), (1, 16)))
    value_weight = normal_values(streams_of[4], (MODEL_DIMENSION, KEY_VALUE_HEADS * HEAD_SIZE), MODEL_DIMENSION ** -0.5, 0.046875, ((0, 16), (1, 16)))
    output_weight = normal_values(streams_of[5], (QUERY_HEADS * HEAD_SIZE, MODEL_DIMENSION), HEAD_SIZE ** -0.5, 0.5, ((0, 16), (1, 16)))
    rotated_key_cache = draw_rotated_key_cache(jax.random.fold_in(streams_of[10], 71), 0)
    stored_value_cache = normal_values(streams_of[7], (TOTAL_ROWS, CACHE_CAPACITY, KEY_VALUE_HEADS * HEAD_SIZE), 1.0, 6.0, ((0, 64), (1, 16)))
    lengths = draw_lengths(jax.random.fold_in(streams_of[10], 71), 0)
    positions = with_ends(jax.random.randint(streams_of[9], (TOTAL_ROWS,), 0, 4096), jax.random.fold_in(streams_of[9], 1), 0, 4095).astype(jnp.int32)
    return {"tokens": tokens, "norm_gain": norm_gain, "w_query": w_query, "key_weight": key_weight, "value_weight": value_weight, "output_weight": output_weight, "rotated_key_cache": rotated_key_cache, "stored_value_cache": stored_value_cache, "lengths": lengths, "positions": positions}


def rotate(values, step_pos):
    full_shape = values.shape
    head_count = full_shape[-1] // HEAD_SIZE
    split_heads = values.reshape(full_shape[:-1] + (head_count, HEAD_SIZE))
    half_dim = HEAD_SIZE // 2
    freq_index = jnp.arange(half_dim, dtype=jnp.float32)
    frequency = jnp.exp(-math.log(500000.0) * 2.0 * freq_index / HEAD_SIZE)
    angles = step_pos[..., None, None] * frequency
    cosine = jnp.cos(angles)
    sines = jnp.sin(angles)
    leading = split_heads[..., :half_dim]
    trailing = split_heads[..., half_dim:]
    rotated = jnp.concatenate([leading * cosine - trailing * sines, trailing * cosine + leading * sines], axis=-1)
    return rotated.reshape(full_shape)

def attend_row(query_rows, appended_keys, appended_values, stored_keys, stored_values, row_length):
    group_width = QUERY_HEADS // KEY_VALUE_HEADS
    score_scale = HEAD_SIZE ** (-0.5)
    decode_steps = query_rows.shape[0]
    query_head_split = query_rows.astype(jnp.float32).reshape(decode_steps, KEY_VALUE_HEADS, group_width, HEAD_SIZE)
    key_tiles = stored_keys.astype(jnp.float32).reshape(N_WIDTH, CONTEXT_PER_SLICE, KEY_VALUE_HEADS, HEAD_SIZE)
    value_tiles = stored_values.astype(jnp.float32).reshape(N_WIDTH, CONTEXT_PER_SLICE, KEY_VALUE_HEADS, HEAD_SIZE)
    scores = jnp.einsum('sgjd,bcgd->sgjbc', query_head_split, key_tiles) * score_scale
    slot_index = jnp.arange(N_WIDTH, dtype=jnp.int32)[:, None] * CONTEXT_PER_SLICE + jnp.arange(CONTEXT_PER_SLICE, dtype=jnp.int32)[None, :]
    valid_slots = (slot_index < row_length)[None, None, None, :, :]
    masked = jnp.where(valid_slots, scores, -1e+30)
    block_max = lax.optimization_barrier(jnp.max(masked, axis=-1))
    weights = jnp.where(valid_slots, jnp.exp(masked - block_max[..., None]), 0.0).astype(jnp.bfloat16)
    block_sum = lax.optimization_barrier(jnp.sum(weights.astype(jnp.float32), axis=-1))
    weighted = jnp.einsum('sgjbc,bcgd->sgjbd', weights.astype(jnp.float32), value_tiles)
    current_keys = appended_keys.astype(jnp.float32).reshape(decode_steps, KEY_VALUE_HEADS, HEAD_SIZE)
    current_values = appended_values.astype(jnp.float32).reshape(decode_steps, KEY_VALUE_HEADS, HEAD_SIZE)
    new_scores = jnp.einsum('sgjd,ugd->sgju', query_head_split, current_keys) * score_scale
    visible = (jnp.arange(decode_steps, dtype=jnp.int32)[None, :] <= jnp.arange(decode_steps, dtype=jnp.int32)[:, None])[:, None, None, :]
    new_masked = jnp.where(visible, new_scores, -1e+30)
    new_max = lax.optimization_barrier(jnp.max(new_masked, axis=-1))
    new_weights = jnp.where(visible, jnp.exp(new_masked - new_max[..., None]), 0.0).astype(jnp.bfloat16)
    new_sum = lax.optimization_barrier(jnp.sum(new_weights.astype(jnp.float32), axis=-1))
    new_weighted = jnp.einsum('sgju,ugd->sgjd', new_weights.astype(jnp.float32), current_values)
    row_peak = jnp.maximum(lax.optimization_barrier(jnp.max(block_max, axis=-1)), new_max)
    factor = jnp.exp(block_max - row_peak[..., None])
    new_factor = jnp.exp(new_max - row_peak)
    denominator = lax.optimization_barrier(jnp.sum(block_sum * factor, axis=-1)) + new_sum * new_factor
    numerator = lax.optimization_barrier(jnp.sum(weighted * factor[..., None], axis=3)) + new_weighted * new_factor[..., None]
    return (numerator / denominator[..., None]).astype(jnp.bfloat16).reshape(decode_steps, QUERY_HEADS * HEAD_SIZE)

def reference(tokens, norm_gain, w_query, key_weight, value_weight, output_weight, rotated_key_cache, stored_value_cache, lengths, positions):
    row_count, decode_steps, model_width = tokens.shape
    as_float = tokens.astype(jnp.float32)
    squares = lax.optimization_barrier(jnp.sum(as_float * as_float, axis=2, keepdims=True))
    inverse = lax.rsqrt(squares / model_width + 1e-05)
    scaled = (as_float * norm_gain.astype(jnp.float32)).astype(jnp.bfloat16).reshape(row_count * decode_steps, model_width)

    def project(matrix):
        return jnp.dot(scaled, matrix, preferred_element_type=jnp.float32).reshape(row_count, decode_steps, -1) * inverse
    step_pos = (positions[:, None] + jnp.arange(decode_steps, dtype=jnp.int32)[None, :]).astype(jnp.float32)
    query_rows = rotate(project(w_query), step_pos).astype(jnp.bfloat16)
    appended_keys = rotate(project(key_weight), step_pos).astype(jnp.bfloat16)
    appended_values = project(value_weight).astype(jnp.bfloat16)

    def per_row(packed):
        return attend_row(*packed)
    attended = lax.map(per_row, (query_rows, appended_keys, appended_values, rotated_key_cache, stored_value_cache, lengths))
    layer_out = jnp.dot(attended.reshape(row_count * decode_steps, QUERY_HEADS * HEAD_SIZE), output_weight, preferred_element_type=jnp.float32)
    return layer_out.astype(jnp.bfloat16).reshape(row_count, decode_steps, -1)
```

```python
import functools
import math

import jax
import jax.numpy as jnp
from jax import lax
from jax.experimental import pallas as pl
from jax.experimental.pallas import tpu as pltpu
from jax.sharding import PartitionSpec as P

MESH = pl.DeviceIdType.MESH
MODEL_DIMENSION = 16384
HEAD_SIZE = 128
N = 16
GROUP = 8
STEPS = 2
ROWS = N * STEPS
SLOTS = 64
EXTENDED = 80
NEGATIVE = -1e30


def wait_bytes(ref, sem):
    pltpu.make_async_copy(ref, ref, sem).wait()


def to_messages(wide, message):
    for row in range(N):
        parts = [wide[pl.ds(STEPS * row + t, GROUP, stride=ROWS), :] for t in range(STEPS)]
        message[row] = jnp.concatenate(parts, axis=0).astype(jnp.bfloat16)


def kernel(
    lengths,
    positions,
    tokens_hbm,
    gain_ref,
    w_query_hbm,
    key_hbm,
    value_hbm,
    w_out_hbm,
    key_cache_hbm,
    value_cache_hbm,
    out_ref,
    tokens,
    w_query,
    w_key,
    w_value,
    w_out,
    keys,
    values,
    flat,
    wide,
    message,
    aux,
    part_in,
    aux_in,
    query_out,
    fresh_out,
    query_in,
    fresh_in,
    fresh_rows,
    block_out,
    stat_wide,
    stat_out,
    block_in,
    stat_in,
    coef,
    head_out,
    head_in,
    head_wide,
    total,
    out_in,
    load_sem,
    send_sem,
    recv_sem,
):
    z = lax.axis_index("width")
    h = lax.axis_index("hidden")

    chunk = 256
    loads = [
        pltpu.make_async_copy(tokens_hbm, tokens, load_sem.at[0]),
        pltpu.make_async_copy(key_hbm, w_key, load_sem.at[1]),
        pltpu.make_async_copy(value_hbm, w_value, load_sem.at[2]),
    ]
    for c in range(4):
        cols = pl.ds(c * chunk, chunk)
        loads.append(
            pltpu.make_async_copy(w_query_hbm.at[:, cols], w_query.at[:, cols], load_sem.at[3 + c])
        )
    loads.append(
        pltpu.make_async_copy(key_cache_hbm.at[0], keys.at[pl.ds(0, SLOTS)], load_sem.at[7])
    )
    loads.append(
        pltpu.make_async_copy(value_cache_hbm.at[0], values.at[pl.ds(0, SLOTS)], load_sem.at[8])
    )
    loads.append(pltpu.make_async_copy(w_out_hbm, w_out, load_sem.at[9]))
    for load in loads:
        load.start()

    barrier = pltpu.get_barrier_semaphore()

    def greet(d, carry):
        pl.semaphore_signal(
            barrier, inc=1, device_id={"width": lax.rem(z + d, N)}, device_id_type=MESH
        )
        pl.semaphore_signal(
            barrier, inc=1, device_id={"hidden": lax.rem(h + d, N)}, device_id_type=MESH
        )
        return carry

    lax.fori_loop(1, N, greet, 0)

    loads[0].wait()
    for row in range(N):
        flat[pl.ds(STEPS * row, STEPS), :] = tokens[row].astype(jnp.float32)
    x = flat[...]
    gain = gain_ref[...].astype(jnp.float32).reshape(1, -1)
    squares = jnp.sum(x * x, axis=1, keepdims=True)
    scaled = (x * gain).astype(jnp.bfloat16)
    loads[1].wait()
    loads[2].wait()
    new_key = jnp.dot(scaled, w_key[...], preferred_element_type=jnp.float32)
    new_value = jnp.dot(scaled, w_value[...], preferred_element_type=jnp.float32)
    fresh = jnp.concatenate([new_key, new_value], axis=1)
    odd = lax.rem(h, 2) == 1
    fresh = jnp.where(odd, pltpu.roll(fresh, 64, 1), fresh)
    spread = jnp.broadcast_to(squares, (ROWS, HEAD_SIZE))
    for row in range(N):
        aux[row, 0:2, :] = fresh[STEPS * row : STEPS * row + STEPS, :]
        aux[row, 2:4, :] = spread[STEPS * row : STEPS * row + STEPS, :]
    for c in range(4):
        loads[3 + c].wait()
        part = jnp.dot(
            scaled, w_query[:, c * chunk : (c + 1) * chunk], preferred_element_type=jnp.float32
        )
        wide[pl.ds(2 * c * ROWS, ROWS), :] = part[:, :HEAD_SIZE]
        wide[pl.ds((2 * c + 1) * ROWS, ROWS), :] = part[:, HEAD_SIZE:]
    to_messages(wide, message)

    pl.semaphore_wait(barrier, 2 * (N - 1))

    def send_part(d, carry):
        to = lax.rem(z + d, N)
        pltpu.make_async_remote_copy(
            message.at[to],
            part_in.at[z],
            send_sem.at[0],
            recv_sem.at[0],
            device_id={"width": to},
            device_id_type=MESH,
        ).start()
        pltpu.make_async_remote_copy(
            aux.at[to],
            aux_in.at[z],
            send_sem.at[1],
            recv_sem.at[1],
            device_id={"width": to},
            device_id_type=MESH,
        ).start()
        return carry

    lax.fori_loop(1, N, send_part, 0)
    pltpu.make_async_copy(message.at[z], part_in.at[z], recv_sem.at[0]).start()
    pltpu.make_async_copy(aux.at[z], aux_in.at[z], recv_sem.at[1]).start()

    lane = lax.broadcasted_iota(jnp.int32, (STEPS, HEAD_SIZE), 1)
    step = lax.broadcasted_iota(jnp.int32, (STEPS, HEAD_SIZE), 0)
    index = jnp.where(lane < 64, lane, lane - 64).astype(jnp.float32)
    frequency = jnp.exp(-math.log(500000.0) * 2.0 * index / HEAD_SIZE)
    angles = (positions[0] + step).astype(jnp.float32) * frequency
    cosine = jnp.cos(angles)
    sine = jnp.where(lane < 64, -jnp.sin(angles), jnp.sin(angles))
    fresh_rows[...] = jnp.zeros_like(fresh_rows)

    wait_bytes(aux_in, recv_sem.at[1])
    wait_bytes(part_in, recv_sem.at[0])
    summed = jnp.sum(aux_in[...], axis=0)
    inverse = lax.rsqrt(summed[2:4] / MODEL_DIMENSION + 1e-05)
    fresh_out[...] = summed[0:2] * inverse
    q = jnp.sum(part_in[...].astype(jnp.float32), axis=0)
    both = jnp.concatenate(
        [jnp.broadcast_to(inverse[t : t + 1], (GROUP, HEAD_SIZE)) for t in range(STEPS)], axis=0
    )
    query_out[...] = (q * both).astype(jnp.bfloat16)

    def broadcast_row(source, target, index):
        def send(d, carry):
            pltpu.make_async_remote_copy(
                source,
                target.at[h],
                send_sem.at[index],
                recv_sem.at[index],
                device_id={"width": lax.rem(z + d, N), "hidden": z},
                device_id_type=MESH,
            ).start()
            return carry

        lax.fori_loop(1, N, send, 0)

        @pl.when(h == z)
        def _():
            pltpu.make_async_copy(source, target.at[h], recv_sem.at[index]).start()

        @pl.when(h != z)
        def _():
            pltpu.make_async_remote_copy(
                source,
                target.at[h],
                send_sem.at[index],
                recv_sem.at[index],
                device_id={"hidden": z},
                device_id_type=MESH,
            ).start()

    @pl.when(h == z)
    def _():
        pltpu.make_async_copy(fresh_out, fresh_in.at[h], recv_sem.at[3]).start()

    @pl.when(h != z)
    def _():
        pltpu.make_async_remote_copy(
            fresh_out,
            fresh_in.at[h],
            send_sem.at[3],
            recv_sem.at[3],
            device_id={"hidden": z},
            device_id_type=MESH,
        ).start()

    broadcast_row(query_out, query_in, 2)

    loads[7].wait()
    loads[8].wait()

    @pl.when(h == z)
    def _():
        wait_bytes(fresh_in, recv_sem.at[3])
        low = lane < 64
        for g in range(8):
            even = fresh_in[2 * g]
            odd_half = fresh_in[2 * g + 1]
            key = jnp.where(low, even, odd_half)
            value = pltpu.roll(jnp.where(low, odd_half, even), 64, 1)
            key = key * cosine + pltpu.roll(key, 64, 1) * sine
            fresh_rows[0, 0:2, g * 128 : (g + 1) * 128] = key
            fresh_rows[1, 0:2, g * 128 : (g + 1) * 128] = value

    keys[SLOTS:EXTENDED, :] = fresh_rows[0].astype(jnp.bfloat16)
    values[SLOTS:EXTENDED, :] = fresh_rows[1].astype(jnp.bfloat16)

    column = lax.broadcasted_iota(jnp.int32, (2 * N, EXTENDED), 1)
    row_step = lax.rem(lax.broadcasted_iota(jnp.int32, (2 * N, EXTENDED), 0) // GROUP, STEPS)
    here = jnp.where(h == z, 1, 0)
    cached = jnp.where(z * SLOTS + column < lengths[0], 1, 0)
    appended = jnp.where(column - SLOTS <= row_step, here, 0)
    valid = jnp.where(column < SLOTS, cached, appended) == 1
    cosines = jnp.concatenate(
        [jnp.broadcast_to(cosine[t : t + 1], (GROUP, HEAD_SIZE)) for t in (0, 1, 0, 1)], axis=0
    )
    sines = jnp.concatenate(
        [jnp.broadcast_to(sine[t : t + 1], (GROUP, HEAD_SIZE)) for t in (0, 1, 0, 1)], axis=0
    )

    wait_bytes(query_in, recv_sem.at[2])
    for g in range(8):
        cols = slice(g * HEAD_SIZE, (g + 1) * HEAD_SIZE)
        q = jnp.concatenate([query_in[2 * g], query_in[2 * g + 1]], axis=0).astype(jnp.float32)
        q = (q * cosines + pltpu.roll(q, 64, 1) * sines).astype(jnp.bfloat16)
        scores = lax.dot_general(
            q, keys[:, cols], (((1,), (1,)), ((), ())), preferred_element_type=jnp.float32
        ) * (HEAD_SIZE**-0.5)
        masked = jnp.where(valid, scores, NEGATIVE)
        block_max = jnp.max(masked, axis=1, keepdims=True)
        weights = jnp.where(valid, jnp.exp(masked - block_max), 0.0).astype(jnp.bfloat16)
        block_sum = jnp.sum(weights.astype(jnp.float32), axis=1, keepdims=True)
        weighted = jnp.dot(weights, values[:, cols], preferred_element_type=jnp.float32)
        filled = block_sum > 0.0
        safe = jnp.where(filled, block_sum, 1.0)
        level = jnp.where(filled, block_max + jnp.log(safe), NEGATIVE)
        block = (weighted / safe).astype(jnp.bfloat16)
        block_out[2 * g] = block[:N]
        block_out[2 * g + 1] = block[N:]
        stat_wide[2 * g * N : 2 * (g + 1) * N, :] = jnp.broadcast_to(level, (2 * N, HEAD_SIZE))
    for half in range(2):
        turned = stat_wide[half * 128 : (half + 1) * 128, :].T
        stat_out[half] = turned[0:1, :]

    def send_block(d, carry):
        to = lax.rem(z + d, N)
        pltpu.make_async_remote_copy(
            stat_out.at[to // GROUP],
            stat_in.at[z],
            send_sem.at[5],
            recv_sem.at[5],
            device_id={"width": to},
            device_id_type=MESH,
        ).start()
        pltpu.make_async_remote_copy(
            block_out.at[to],
            block_in.at[z],
            send_sem.at[4],
            recv_sem.at[4],
            device_id={"width": to},
            device_id_type=MESH,
        ).start()
        return carry

    lax.fori_loop(1, N, send_block, 0)
    pltpu.make_async_copy(stat_out.at[z // GROUP], stat_in.at[z], recv_sem.at[5]).start()
    pltpu.make_async_copy(block_out.at[z], block_in.at[z], recv_sem.at[4]).start()
    coef[...] = jnp.zeros_like(coef)

    wait_bytes(stat_in, recv_sem.at[5])
    levels = [stat_in[i] for i in range(N)]
    peak = functools.reduce(jnp.maximum, levels)
    factors = [jnp.exp(level - peak) for level in levels]
    denominator = functools.reduce(jnp.add, factors)
    for i in range(N):
        coef[i : i + 1, :] = factors[i] / denominator
    coef[...] = coef[...].T
    mine = coef[pl.ds(pl.multiple_of(lax.rem(z, GROUP) * N, N), N), :]
    wait_bytes(block_in, recv_sem.at[4])
    merged = block_in[0].astype(jnp.float32) * mine[:, 0:1]
    for i in range(1, N):
        merged = merged + block_in[i].astype(jnp.float32) * mine[:, i : i + 1]
    head_out[...] = merged.astype(jnp.bfloat16)

    broadcast_row(head_out, head_in, 6)
    loads[9].wait()
    wait_bytes(head_in, recv_sem.at[6])
    head_wide[...] = head_in[...].astype(jnp.float32).reshape(N * N, HEAD_SIZE)
    attended = jnp.concatenate(
        [head_wide[pl.ds(j, ROWS, stride=GROUP), :].astype(jnp.bfloat16) for j in range(GROUP)],
        axis=1,
    )
    for c in range(4):
        part = jnp.dot(
            attended, w_out[:, c * chunk : (c + 1) * chunk], preferred_element_type=jnp.float32
        )
        wide[pl.ds(2 * c * ROWS, ROWS), :] = part[:, :HEAD_SIZE]
        wide[pl.ds((2 * c + 1) * ROWS, ROWS), :] = part[:, HEAD_SIZE:]
    wait_bytes(message.at[pl.ds(0, N - 1)], send_sem.at[0])
    to_messages(wide, message)

    def send_out(d, carry):
        to = lax.rem(h + d, N)
        pltpu.make_async_remote_copy(
            message.at[to],
            out_in.at[h],
            send_sem.at[7],
            recv_sem.at[7],
            device_id={"hidden": to},
            device_id_type=MESH,
        ).start()
        return carry

    lax.fori_loop(1, N, send_out, 0)
    pltpu.make_async_copy(message.at[h], out_in.at[h], recv_sem.at[7]).start()

    wait_bytes(aux.at[pl.ds(0, N - 1)], send_sem.at[1])
    wait_bytes(query_in.at[pl.ds(0, N - 1)], send_sem.at[2])
    wait_bytes(block_in.at[pl.ds(0, N - 1)], send_sem.at[4])
    wait_bytes(stat_in.at[pl.ds(0, N - 1)], send_sem.at[5])
    wait_bytes(head_in.at[pl.ds(0, N - 1)], send_sem.at[6])

    @pl.when(h != z)
    def _():
        wait_bytes(query_in.at[0], send_sem.at[2])
        wait_bytes(fresh_in.at[0], send_sem.at[3])
        wait_bytes(head_in.at[0], send_sem.at[6])

    wait_bytes(out_in, recv_sem.at[7])
    total[...] = jnp.sum(out_in[...].astype(jnp.float32), axis=0)
    for c in range(GROUP):
        both_steps = total[pl.ds(c, STEPS, stride=GROUP), :]
        out_ref[0, :, c * HEAD_SIZE : (c + 1) * HEAD_SIZE] = both_steps.astype(jnp.bfloat16)
    wait_bytes(out_in.at[pl.ds(0, N - 1)], send_sem.at[7])


def local(
    tokens,
    norm_gain,
    w_query,
    key_weight,
    value_weight,
    output_weight,
    rotated_key_cache,
    stored_value_cache,
    lengths,
    positions,
):
    smem = pl.BlockSpec(memory_space=pltpu.SMEM)
    vmem = pl.BlockSpec(memory_space=pltpu.VMEM)
    anywhere = pl.BlockSpec(memory_space=pl.ANY)
    half, full = jnp.bfloat16, jnp.float32
    features = tokens.shape[2]
    columns = w_query.shape[1]
    scratch = [
        pltpu.VMEM(tokens.shape, half),
        pltpu.VMEM(w_query.shape, half),
        pltpu.VMEM(key_weight.shape, half),
        pltpu.VMEM(value_weight.shape, half),
        pltpu.VMEM(output_weight.shape, half),
        pltpu.VMEM((EXTENDED, 1024), half),
        pltpu.VMEM((EXTENDED, 1024), half),
        pltpu.VMEM((ROWS, features), full),
        pltpu.VMEM((GROUP * ROWS, HEAD_SIZE), full),
        pltpu.VMEM((N, N, HEAD_SIZE), half),
        pltpu.VMEM((N, 4, HEAD_SIZE), full),
        pltpu.VMEM((N, N, HEAD_SIZE), half),
        pltpu.VMEM((N, 4, HEAD_SIZE), full),
        pltpu.VMEM((N, HEAD_SIZE), half),
        pltpu.VMEM((STEPS, HEAD_SIZE), full),
        pltpu.VMEM((N, N, HEAD_SIZE), half),
        pltpu.VMEM((N, STEPS, HEAD_SIZE), full),
        pltpu.VMEM((2, N, 1024), full),
        pltpu.VMEM((N, N, HEAD_SIZE), half),
        pltpu.VMEM((N * N, HEAD_SIZE), full),
        pltpu.VMEM((2, 1, HEAD_SIZE), full),
        pltpu.VMEM((N, N, HEAD_SIZE), half),
        pltpu.VMEM((N, 1, HEAD_SIZE), full),
        pltpu.VMEM((HEAD_SIZE, HEAD_SIZE), full),
        pltpu.VMEM((N, HEAD_SIZE), half),
        pltpu.VMEM((N, N, HEAD_SIZE), half),
        pltpu.VMEM((N * N, HEAD_SIZE), full),
        pltpu.VMEM((N, HEAD_SIZE), full),
        pltpu.VMEM((N, N, HEAD_SIZE), half),
        pltpu.SemaphoreType.DMA((10,)),
        pltpu.SemaphoreType.DMA((8,)),
        pltpu.SemaphoreType.DMA((8,)),
    ]
    return pl.pallas_call(
        kernel,
        out_shape=jax.ShapeDtypeStruct((1, STEPS, columns), half),
        in_specs=[smem, smem, anywhere, vmem] + [anywhere] * 6,
        out_specs=vmem,
        scratch_shapes=scratch,
        compiler_params=pltpu.CompilerParams(
            collective_id=0, has_side_effects=True, vmem_limit_bytes=48 * 2**20
        ),
        name="decode_block",
    )(
        lengths,
        positions,
        tokens,
        norm_gain,
        w_query,
        key_weight,
        value_weight,
        output_weight,
        rotated_key_cache,
        stored_value_cache,
    )


def solution(mesh):
    return jax.shard_map(
        local,
        mesh=mesh,
        in_specs=(
            P("batch", None, "width"),
            P("width"),
            P("width", "hidden"),
            P("width", "hidden"),
            P("width", "hidden"),
            P("hidden", "width"),
            P(("batch", "hidden"), "width", None),
            P(("batch", "hidden"), "width", None),
            P(("batch", "hidden")),
            P(("batch", "hidden")),
        ),
        out_specs=P(("batch", "hidden"), None, "width"),
        check_vma=False,
    )
```

```python
import functools
import math

import jax
import jax.numpy as jnp
from jax import lax
from jax.experimental import pallas as pl
from jax.experimental.pallas import tpu as pltpu
from jax.sharding import PartitionSpec as P

MESH = pl.DeviceIdType.MESH
MODEL_DIMENSION = 16384
HEAD_SIZE = 128
N = 16
GROUP = 8
STEPS = 2
ROWS = N * STEPS
SLOTS = 64
EXTENDED = 80
NEGATIVE = -1e30


def wait_bytes(ref, sem):
    pltpu.make_async_copy(ref, ref, sem).wait()


def put(source, target, send, recv, **device):
    return pltpu.make_async_remote_copy(
        source, target, send, recv, device_id=device, device_id_type=MESH
    )


def far_first(i):
    return N // 2 + ((i + 1) // 2) * (2 * lax.rem(i, 2) - 1)


def to_messages(wide, message):
    for row in range(N):
        parts = [wide[pl.ds(STEPS * row + t, GROUP, stride=ROWS), :] for t in range(STEPS)]
        message[row] = jnp.concatenate(parts, axis=0).astype(jnp.bfloat16)


def kernel(
    lengths,
    positions,
    tokens_hbm,
    gain_hbm,
    w_query_hbm,
    key_hbm,
    value_hbm,
    w_out_hbm,
    key_cache_hbm,
    value_cache_hbm,
    out_ref,
    tokens,
    gain_ref,
    w_query,
    w_key,
    w_value,
    w_out,
    keys,
    values,
    flat,
    wide,
    table_out,
    table_in,
    message,
    aux,
    part_in,
    aux_in,
    query_out,
    fresh_out,
    query_in,
    fresh_in,
    fresh_rows,
    block_out,
    stat_wide,
    stat_out,
    block_in,
    stat_in,
    coef,
    head_out,
    head_in,
    head_wide,
    total,
    out_in,
    load_sem,
    send_sem,
    recv_sem,
):
    z = lax.axis_index("width")
    h = lax.axis_index("hidden")

    chunk = 256
    loads = [
        pltpu.make_async_copy(tokens_hbm, tokens, load_sem.at[0]),
        pltpu.make_async_copy(key_hbm, w_key, load_sem.at[1]),
        pltpu.make_async_copy(value_hbm, w_value, load_sem.at[2]),
    ]
    load_gain = pltpu.make_async_copy(gain_hbm, gain_ref, load_sem.at[10])
    for c in range(4):
        cols = pl.ds(c * chunk, chunk)
        loads.append(
            pltpu.make_async_copy(w_query_hbm.at[:, cols], w_query.at[:, cols], load_sem.at[3 + c])
        )
    loads.append(
        pltpu.make_async_copy(key_cache_hbm.at[0], keys.at[pl.ds(0, SLOTS)], load_sem.at[7])
    )
    loads.append(
        pltpu.make_async_copy(value_cache_hbm.at[0], values.at[pl.ds(0, SLOTS)], load_sem.at[8])
    )
    loads.append(pltpu.make_async_copy(w_out_hbm, w_out, load_sem.at[9]))
    load_gain.start()
    for load in loads:
        load.start()

    barrier = pltpu.get_barrier_semaphore()

    def greet(i, carry):
        d = far_first(i)
        pl.semaphore_signal(
            barrier, inc=1, device_id={"width": lax.rem(z + d, N)}, device_id_type=MESH
        )
        pl.semaphore_signal(
            barrier, inc=1, device_id={"hidden": lax.rem(h + d, N)}, device_id_type=MESH
        )
        return carry

    lax.fori_loop(0, N - 1, greet, 0)

    lane = lax.broadcasted_iota(jnp.int32, (STEPS, HEAD_SIZE), 1)
    step = lax.broadcasted_iota(jnp.int32, (STEPS, HEAD_SIZE), 0)
    index = jnp.where(lane < 64, lane, lane - 64).astype(jnp.float32)
    frequency = jnp.exp(-math.log(500000.0) * 2.0 * index / HEAD_SIZE)
    angles = (positions[0] + step).astype(jnp.float32) * frequency
    cosine = jnp.cos(angles)
    sine = jnp.where(lane < 64, -jnp.sin(angles), jnp.sin(angles))
    table_out[0] = cosine
    table_out[1] = sine
    fresh_rows[...] = jnp.zeros_like(fresh_rows)
    coef[...] = jnp.zeros_like(coef)

    loads[0].wait()
    load_gain.wait()
    for row in range(N):
        flat[pl.ds(STEPS * row, STEPS), :] = tokens[row].astype(jnp.float32)
    x = flat[...]
    gain = gain_ref[...].astype(jnp.float32).reshape(1, -1)
    squares = jnp.sum(x * x, axis=1, keepdims=True)
    scaled = (x * gain).astype(jnp.bfloat16)
    loads[1].wait()
    loads[2].wait()
    by_rows = (((1,), (1,)), ((), ()))
    new_key = lax.dot_general(scaled, w_key[...], by_rows, preferred_element_type=jnp.float32)
    new_value = lax.dot_general(scaled, w_value[...], by_rows, preferred_element_type=jnp.float32)
    fresh = jnp.concatenate([new_key, new_value], axis=1)
    odd = lax.rem(h, 2) == 1
    fresh = jnp.where(odd, pltpu.roll(fresh, 64, 1), fresh)
    spread = jnp.broadcast_to(squares, (ROWS, HEAD_SIZE))
    for row in range(N):
        aux[row, 0:2, :] = fresh[STEPS * row : STEPS * row + STEPS, :]
        aux[row, 2:4, :] = spread[STEPS * row : STEPS * row + STEPS, :]
    for c in range(4):
        loads[3 + c].wait()
        part = jnp.dot(
            scaled, w_query[:, c * chunk : (c + 1) * chunk], preferred_element_type=jnp.float32
        )
        wide[pl.ds(2 * c * ROWS, ROWS), :] = part[:, :HEAD_SIZE]
        wide[pl.ds((2 * c + 1) * ROWS, ROWS), :] = part[:, HEAD_SIZE:]
    to_messages(wide, message)

    pl.semaphore_wait(barrier, 2 * (N - 1))

    @pl.when(h == z)
    def _():
        def send_table(i, carry):
            put(
                table_out,
                table_in,
                send_sem.at[8],
                recv_sem.at[8],
                hidden=lax.rem(h + far_first(i), N),
            ).start()
            return carry

        lax.fori_loop(0, N - 1, send_table, 0)
        pltpu.make_async_copy(table_out, table_in, recv_sem.at[8]).start()

    def send_part(i, carry):
        to = lax.rem(z + far_first(i), N)
        put(message.at[to], part_in.at[z], send_sem.at[0], recv_sem.at[0], width=to).start()
        put(aux.at[to], aux_in.at[z], send_sem.at[1], recv_sem.at[1], width=to).start()
        return carry

    lax.fori_loop(0, N - 1, send_part, 0)
    pltpu.make_async_copy(message.at[z], part_in.at[z], recv_sem.at[0]).start()
    pltpu.make_async_copy(aux.at[z], aux_in.at[z], recv_sem.at[1]).start()

    wait_bytes(table_in, recv_sem.at[8])
    cosines, sines = [
        jnp.concatenate(
            [jnp.broadcast_to(table_in[k, t : t + 1], (GROUP, HEAD_SIZE)) for t in range(STEPS)],
            axis=0,
        )
        for k in range(2)
    ]
    wait_bytes(aux_in, recv_sem.at[1])
    wait_bytes(part_in, recv_sem.at[0])
    summed = jnp.sum(aux_in[...], axis=0)
    inverse = lax.rsqrt(summed[2:4] / MODEL_DIMENSION + 1e-05)
    fresh_out[...] = summed[0:2] * inverse
    q = jnp.sum(part_in[...].astype(jnp.float32), axis=0)
    both = jnp.concatenate(
        [jnp.broadcast_to(inverse[t : t + 1], (GROUP, HEAD_SIZE)) for t in range(STEPS)], axis=0
    )
    q = q * both
    query_out[...] = (q * cosines + pltpu.roll(q, 64, 1) * sines).astype(jnp.bfloat16)

    def broadcast_row(source, target, index):
        send, recv = send_sem.at[index], recv_sem.at[index]

        def send_row(i, carry):
            to = lax.rem(z + far_first(i), N)
            put(source, target.at[h], send, recv, width=to, hidden=z).start()
            return carry

        lax.fori_loop(0, N - 1, send_row, 0)
        send_one(source, target, index)

    def send_one(source, target, index):
        @pl.when(h == z)
        def _():
            pltpu.make_async_copy(source, target.at[h], recv_sem.at[index]).start()

        @pl.when(h != z)
        def _():
            put(
                source, target.at[h], send_sem.at[index], recv_sem.at[index], hidden=z
            ).start()

    broadcast_row(query_out, query_in, 2)
    send_one(fresh_out, fresh_in, 3)

    loads[7].wait()
    loads[8].wait()

    @pl.when(h == z)
    def _():
        wait_bytes(fresh_in, recv_sem.at[3])
        low = lane < 64
        for g in range(8):
            even = fresh_in[2 * g]
            odd_half = fresh_in[2 * g + 1]
            key = jnp.where(low, even, odd_half)
            value = pltpu.roll(jnp.where(low, odd_half, even), 64, 1)
            key = key * cosine + pltpu.roll(key, 64, 1) * sine
            fresh_rows[0, 0:2, g * 128 : (g + 1) * 128] = key
            fresh_rows[1, 0:2, g * 128 : (g + 1) * 128] = value

    keys[SLOTS:EXTENDED, :] = fresh_rows[0].astype(jnp.bfloat16)
    values[SLOTS:EXTENDED, :] = fresh_rows[1].astype(jnp.bfloat16)

    column = lax.broadcasted_iota(jnp.int32, (2 * N, EXTENDED), 1)
    row_step = lax.rem(lax.broadcasted_iota(jnp.int32, (2 * N, EXTENDED), 0) // GROUP, STEPS)
    here = jnp.where(h == z, 1, 0)
    cached = jnp.where(z * SLOTS + column < lengths[0], 1, 0)
    appended = jnp.where(column - SLOTS <= row_step, here, 0)
    valid = jnp.where(column < SLOTS, cached, appended) == 1
    wait_bytes(query_in, recv_sem.at[2])
    for g in range(8):
        cols = slice(g * HEAD_SIZE, (g + 1) * HEAD_SIZE)
        q = jnp.concatenate([query_in[2 * g], query_in[2 * g + 1]], axis=0)
        scores = lax.dot_general(
            q, keys[:, cols], by_rows, preferred_element_type=jnp.float32
        ) * (HEAD_SIZE**-0.5)
        masked = jnp.where(valid, scores, NEGATIVE)
        block_max = jnp.max(masked, axis=1, keepdims=True)
        weights = jnp.where(valid, jnp.exp(masked - block_max), 0.0).astype(jnp.bfloat16)
        block_sum = jnp.sum(weights.astype(jnp.float32), axis=1, keepdims=True)
        weighted = jnp.dot(weights, values[:, cols], preferred_element_type=jnp.float32)
        filled = block_sum > 0.0
        safe = jnp.where(filled, block_sum, 1.0)
        level = jnp.where(filled, block_max + jnp.log(safe), NEGATIVE)
        block = (weighted / safe).astype(jnp.bfloat16)
        block_out[2 * g] = block[:N]
        block_out[2 * g + 1] = block[N:]
        stat_wide[2 * g * N : 2 * (g + 1) * N, :] = jnp.broadcast_to(level, (2 * N, HEAD_SIZE))
    for half in range(2):
        turned = stat_wide[half * 128 : (half + 1) * 128, :].T
        stat_out[half] = turned[0:1, :]

    def send_block(i, carry):
        to = lax.rem(z + far_first(i), N)
        stat = stat_out.at[to // GROUP]
        put(stat, stat_in.at[z], send_sem.at[5], recv_sem.at[5], width=to).start()
        put(block_out.at[to], block_in.at[z], send_sem.at[4], recv_sem.at[4], width=to).start()
        return carry

    lax.fori_loop(0, N - 1, send_block, 0)
    pltpu.make_async_copy(stat_out.at[z // GROUP], stat_in.at[z], recv_sem.at[5]).start()
    pltpu.make_async_copy(block_out.at[z], block_in.at[z], recv_sem.at[4]).start()

    wait_bytes(stat_in, recv_sem.at[5])
    levels = [stat_in[i] for i in range(N)]
    peak = functools.reduce(jnp.maximum, levels)
    factors = [jnp.exp(level - peak) for level in levels]
    denominator = functools.reduce(jnp.add, factors)
    for i in range(N):
        coef[i : i + 1, :] = factors[i] / denominator
    coef[...] = coef[...].T
    mine = coef[pl.ds(pl.multiple_of(lax.rem(z, GROUP) * N, N), N), :]
    wait_bytes(block_in, recv_sem.at[4])
    merged = block_in[0].astype(jnp.float32) * mine[:, 0:1]
    for i in range(1, N):
        merged = merged + block_in[i].astype(jnp.float32) * mine[:, i : i + 1]
    head_out[...] = merged.astype(jnp.bfloat16)

    broadcast_row(head_out, head_in, 6)
    loads[9].wait()
    wait_bytes(head_in, recv_sem.at[6])
    head_wide[...] = head_in[...].astype(jnp.float32).reshape(N * N, HEAD_SIZE)
    attended = jnp.concatenate(
        [head_wide[pl.ds(j, ROWS, stride=GROUP), :].astype(jnp.bfloat16) for j in range(GROUP)],
        axis=1,
    )
    for c in range(4):
        part = jnp.dot(
            attended, w_out[:, c * chunk : (c + 1) * chunk], preferred_element_type=jnp.float32
        )
        wide[pl.ds(2 * c * ROWS, ROWS), :] = part[:, :HEAD_SIZE]
        wide[pl.ds((2 * c + 1) * ROWS, ROWS), :] = part[:, HEAD_SIZE:]
    wait_bytes(message.at[pl.ds(0, N - 1)], send_sem.at[0])
    to_messages(wide, message)

    def send_out(i, carry):
        to = lax.rem(h + far_first(i), N)
        put(message.at[to], out_in.at[h], send_sem.at[7], recv_sem.at[7], hidden=to).start()
        return carry

    lax.fori_loop(0, N - 1, send_out, 0)
    pltpu.make_async_copy(message.at[h], out_in.at[h], recv_sem.at[7]).start()

    wait_bytes(aux.at[pl.ds(0, N - 1)], send_sem.at[1])
    wait_bytes(query_in.at[pl.ds(0, N - 1)], send_sem.at[2])
    wait_bytes(block_in.at[pl.ds(0, N - 1)], send_sem.at[4])
    wait_bytes(stat_in.at[pl.ds(0, N - 1)], send_sem.at[5])
    wait_bytes(head_in.at[pl.ds(0, N - 1)], send_sem.at[6])

    @pl.when(h == z)
    def _():
        for _ in range(N - 1):
            wait_bytes(table_out, send_sem.at[8])

    @pl.when(h != z)
    def _():
        wait_bytes(query_in.at[0], send_sem.at[2])
        wait_bytes(fresh_in.at[0], send_sem.at[3])
        wait_bytes(head_in.at[0], send_sem.at[6])

    wait_bytes(out_in, recv_sem.at[7])
    total[...] = jnp.sum(out_in[...].astype(jnp.float32), axis=0)
    for c in range(GROUP):
        both_steps = total[pl.ds(c, STEPS, stride=GROUP), :]
        out_ref[0, :, c * HEAD_SIZE : (c + 1) * HEAD_SIZE] = both_steps.astype(jnp.bfloat16)
    wait_bytes(out_in.at[pl.ds(0, N - 1)], send_sem.at[7])


def local(
    tokens,
    norm_gain,
    w_query,
    key_weight,
    value_weight,
    output_weight,
    rotated_key_cache,
    stored_value_cache,
    lengths,
    positions,
):
    smem = pl.BlockSpec(memory_space=pltpu.SMEM)
    vmem = pl.BlockSpec(memory_space=pltpu.VMEM)
    hbm = pl.BlockSpec(memory_space=pltpu.HBM)
    half, full = jnp.bfloat16, jnp.float32
    features = tokens.shape[2]
    columns = w_query.shape[1]
    scratch = [
        pltpu.VMEM(tokens.shape, half),
        pltpu.VMEM(norm_gain.shape, half),
        pltpu.VMEM(w_query.shape, half),
        pltpu.VMEM(key_weight.shape[::-1], half),
        pltpu.VMEM(value_weight.shape[::-1], half),
        pltpu.VMEM(output_weight.shape, half),
        pltpu.VMEM((EXTENDED, 1024), half),
        pltpu.VMEM((EXTENDED, 1024), half),
        pltpu.VMEM((ROWS, features), full),
        pltpu.VMEM((GROUP * ROWS, HEAD_SIZE), full),
        pltpu.VMEM((2, STEPS, HEAD_SIZE), full),
        pltpu.VMEM((2, STEPS, HEAD_SIZE), full),
        pltpu.VMEM((N, N, HEAD_SIZE), half),
        pltpu.VMEM((N, 4, HEAD_SIZE), full),
        pltpu.VMEM((N, N, HEAD_SIZE), half),
        pltpu.VMEM((N, 4, HEAD_SIZE), full),
        pltpu.VMEM((N, HEAD_SIZE), half),
        pltpu.VMEM((STEPS, HEAD_SIZE), full),
        pltpu.VMEM((N, N, HEAD_SIZE), half),
        pltpu.VMEM((N, STEPS, HEAD_SIZE), full),
        pltpu.VMEM((2, N, 1024), full),
        pltpu.VMEM((N, N, HEAD_SIZE), half),
        pltpu.VMEM((N * N, HEAD_SIZE), full),
        pltpu.VMEM((2, 1, HEAD_SIZE), full),
        pltpu.VMEM((N, N, HEAD_SIZE), half),
        pltpu.VMEM((N, 1, HEAD_SIZE), full),
        pltpu.VMEM((HEAD_SIZE, HEAD_SIZE), full),
        pltpu.VMEM((N, HEAD_SIZE), half),
        pltpu.VMEM((N, N, HEAD_SIZE), half),
        pltpu.VMEM((N * N, HEAD_SIZE), full),
        pltpu.VMEM((N, HEAD_SIZE), full),
        pltpu.VMEM((N, N, HEAD_SIZE), half),
        pltpu.SemaphoreType.DMA((11,)),
        pltpu.SemaphoreType.DMA((9,)),
        pltpu.SemaphoreType.DMA((9,)),
    ]
    return pl.pallas_call(
        kernel,
        out_shape=jax.ShapeDtypeStruct((1, STEPS, columns), half),
        in_specs=[smem, smem] + [hbm] * 8,
        out_specs=vmem,
        scratch_shapes=scratch,
        compiler_params=pltpu.CompilerParams(
            collective_id=0, has_side_effects=True, vmem_limit_bytes=60 * 2**20
        ),
        name="decode_block",
    )(
        lengths,
        positions,
        tokens,
        norm_gain,
        w_query,
        key_weight.T,
        value_weight.T,
        output_weight,
        rotated_key_cache,
        stored_value_cache,
    )


def solution(mesh):
    return jax.shard_map(
        local,
        mesh=mesh,
        in_specs=(
            P("batch", None, "width"),
            P("width"),
            P("width", "hidden"),
            P("width", "hidden"),
            P("width", "hidden"),
            P("hidden", "width"),
            P(("batch", "hidden"), "width", None),
            P(("batch", "hidden"), "width", None),
            P(("batch", "hidden")),
            P(("batch", "hidden")),
        ),
        out_specs=P(("batch", "hidden"), None, "width"),
        check_vma=False,
    )
```

```python
import functools
import math

import jax
import jax.numpy as jnp
from jax import lax
from jax.experimental import pallas as pl
from jax.experimental.pallas import tpu as pltpu
from jax.sharding import PartitionSpec as P

MESH = pl.DeviceIdType.MESH
MODEL_DIMENSION = 16384
HEAD_SIZE = 128
N = 16
GROUP = 8
STEPS = 2
ROWS = N * STEPS
SLOTS = 64
SUMS = 8
PAIR = N // SUMS
FIRST_MERGE = 12
EXTENDED = 80
NEGATIVE = -1e30


def wait_bytes(ref, sem):
    pltpu.make_async_copy(ref, ref, sem).wait()


def put(source, target, send, recv, **device):
    return pltpu.make_async_remote_copy(
        source, target, send, recv, device_id=device, device_id_type=MESH
    )


def far_first(i):
    return N // 2 + ((i + 1) // 2) * (2 * lax.rem(i, 2) - 1)


def to_messages(wide, message):
    for row in range(N):
        parts = [wide[pl.ds(STEPS * row + t, GROUP, stride=ROWS), :] for t in range(STEPS)]
        message[row] = jnp.concatenate(parts, axis=0).astype(jnp.bfloat16)


def kernel(
    lengths,
    positions,
    tokens_hbm,
    gain_hbm,
    w_query_hbm,
    key_hbm,
    value_hbm,
    w_out_hbm,
    key_cache_hbm,
    value_cache_hbm,
    out_ref,
    tokens,
    gain_ref,
    w_query,
    w_key,
    w_value,
    w_out,
    keys,
    values,
    flat,
    wide,
    table_out,
    table_in,
    message,
    aux,
    part_in,
    aux_in,
    query_out,
    fresh_out,
    query_in,
    fresh_in,
    fresh_rows,
    block_out,
    stat_wide,
    stat_out,
    block_in,
    stat_in,
    coef,
    head_out,
    head_in,
    head_wide,
    total,
    out_in,
    load_sem,
    send_sem,
    recv_sem,
):
    z = lax.axis_index("width")
    h = lax.axis_index("hidden")
    sums_here = z < SUMS
    place = lax.rem(z + N - FIRST_MERGE, N)
    merges_here = place < SUMS

    chunk = 256
    loads = [
        pltpu.make_async_copy(tokens_hbm, tokens, load_sem.at[0]),
        pltpu.make_async_copy(key_hbm, w_key, load_sem.at[1]),
        pltpu.make_async_copy(value_hbm, w_value, load_sem.at[2]),
    ]
    load_gain = pltpu.make_async_copy(gain_hbm, gain_ref, load_sem.at[10])
    for c in range(4):
        cols = pl.ds(c * chunk, chunk)
        loads.append(
            pltpu.make_async_copy(w_query_hbm.at[:, cols], w_query.at[:, cols], load_sem.at[3 + c])
        )
    loads.append(
        pltpu.make_async_copy(key_cache_hbm.at[0], keys.at[pl.ds(0, SLOTS)], load_sem.at[7])
    )
    loads.append(
        pltpu.make_async_copy(value_cache_hbm.at[0], values.at[pl.ds(0, SLOTS)], load_sem.at[8])
    )
    loads.append(pltpu.make_async_copy(w_out_hbm, w_out, load_sem.at[9]))
    load_gain.start()
    for load in loads:
        load.start()

    barrier = pltpu.get_barrier_semaphore()

    def greet_width(i, carry):
        to = lax.rem(z + far_first(i), N)
        pl.semaphore_signal(barrier, inc=1, device_id={"width": to}, device_id_type=MESH)
        return carry

    def greet_hidden(i, carry):
        to = lax.rem(h + far_first(i), N)
        pl.semaphore_signal(barrier, inc=1, device_id={"hidden": to}, device_id_type=MESH)
        return carry

    @pl.when(sums_here)
    def _():
        lax.fori_loop(0, N - 1, greet_width, 0)

    lax.fori_loop(0, N - 1, greet_hidden, 0)

    lane = lax.broadcasted_iota(jnp.int32, (STEPS, HEAD_SIZE), 1)
    step = lax.broadcasted_iota(jnp.int32, (STEPS, HEAD_SIZE), 0)
    index = jnp.where(lane < 64, lane, lane - 64).astype(jnp.float32)
    frequency = jnp.exp(-math.log(500000.0) * 2.0 * index / HEAD_SIZE)
    angles = (positions[0] + step).astype(jnp.float32) * frequency
    cosine = jnp.cos(angles)
    sine = jnp.where(lane < 64, -jnp.sin(angles), jnp.sin(angles))
    table_out[0] = cosine
    table_out[1] = sine
    fresh_rows[...] = jnp.zeros_like(fresh_rows)
    coef[...] = jnp.zeros_like(coef)

    loads[0].wait()
    load_gain.wait()
    for row in range(N):
        flat[pl.ds(STEPS * row, STEPS), :] = tokens[row].astype(jnp.float32)
    x = flat[...]
    gain = gain_ref[...].astype(jnp.float32).reshape(1, -1)
    squares = jnp.sum(x * x, axis=1, keepdims=True)
    scaled = (x * gain).astype(jnp.bfloat16)
    loads[1].wait()
    loads[2].wait()
    by_rows = (((1,), (1,)), ((), ()))
    new_key = lax.dot_general(scaled, w_key[...], by_rows, preferred_element_type=jnp.float32)
    new_value = lax.dot_general(scaled, w_value[...], by_rows, preferred_element_type=jnp.float32)
    fresh = jnp.concatenate([new_key, new_value], axis=1)
    odd = lax.rem(h, 2) == 1
    fresh = jnp.where(odd, pltpu.roll(fresh, 64, 1), fresh)
    spread = jnp.broadcast_to(squares, (ROWS, HEAD_SIZE))
    for row in range(N):
        aux[row, 0:2, :] = fresh[STEPS * row : STEPS * row + STEPS, :]
        aux[row, 2:4, :] = spread[STEPS * row : STEPS * row + STEPS, :]
    for c in range(4):
        loads[3 + c].wait()
        part = jnp.dot(
            scaled, w_query[:, c * chunk : (c + 1) * chunk], preferred_element_type=jnp.float32
        )
        wide[pl.ds(2 * c * ROWS, ROWS), :] = part[:, :HEAD_SIZE]
        wide[pl.ds((2 * c + 1) * ROWS, ROWS), :] = part[:, HEAD_SIZE:]
    to_messages(wide, message)

    pl.semaphore_wait(barrier, N - 1 + SUMS - jnp.where(sums_here, 1, 0))

    @pl.when(h // PAIR == z)
    def _():
        mine = table_in.at[lax.rem(h, PAIR)]

        def send_table(i, carry):
            to = lax.rem(h + far_first(i), N)
            put(table_out, mine, send_sem.at[8], recv_sem.at[8], hidden=to).start()
            return carry

        lax.fori_loop(0, N - 1, send_table, 0)
        pltpu.make_async_copy(table_out, mine, recv_sem.at[8]).start()

    def send_part(i, carry):
        to = lax.rem(z + far_first(i), N)

        @pl.when(to < SUMS)
        def _():
            rows = pl.ds(PAIR * to, PAIR)
            put(message.at[rows], part_in.at[z], send_sem.at[0], recv_sem.at[0], width=to).start()
            put(aux.at[rows], aux_in.at[z], send_sem.at[1], recv_sem.at[1], width=to).start()

        return carry

    lax.fori_loop(0, N - 1, send_part, 0)

    def broadcast_pair(source, target, index, where, nearest):
        send, recv = send_sem.at[index], recv_sem.at[index]

        def send_row(i, carry):
            to = i if nearest else lax.rem(z + far_first(i), N)
            for k in range(PAIR):
                other = PAIR * where + k
                here = jnp.logical_and(to == z, other == h)

                @pl.when(here)
                def _():
                    pltpu.make_async_copy(source.at[k], target.at[h], recv).start()

                @pl.when(jnp.logical_not(here))
                def _():
                    put(source.at[k], target.at[h], send, recv, width=to, hidden=other).start()

            return carry

        lax.fori_loop(0, N, send_row, 0)

    @pl.when(sums_here)
    def _():
        rows = pl.ds(PAIR * z, PAIR)
        pltpu.make_async_copy(message.at[rows], part_in.at[z], recv_sem.at[0]).start()
        pltpu.make_async_copy(aux.at[rows], aux_in.at[z], recv_sem.at[1]).start()
        wait_bytes(table_in, recv_sem.at[8])
        wait_bytes(aux_in, recv_sem.at[1])
        summed = jnp.sum(aux_in[...], axis=0)
        wait_bytes(part_in, recv_sem.at[0])
        sums = jnp.sum(part_in[...].astype(jnp.float32), axis=0)
        for k in range(PAIR):
            inverse = lax.rsqrt(summed[k, 2:4] / MODEL_DIMENSION + 1e-05)
            fresh_out[k] = summed[k, 0:2] * inverse
            scale, cosines, sines = [
                jnp.concatenate(
                    [jnp.broadcast_to(a[t : t + 1], (GROUP, HEAD_SIZE)) for t in range(STEPS)],
                    axis=0,
                )
                for a in (inverse, table_in[k, 0], table_in[k, 1])
            ]
            q = sums[k] * scale
            query_out[k] = (q * cosines + pltpu.roll(q, 64, 1) * sines).astype(jnp.bfloat16)
        broadcast_pair(query_out, query_in, 2, z, False)
        for k in range(PAIR):
            row = PAIR * z + k

            @pl.when(row == h)
            def _():
                pltpu.make_async_copy(fresh_out.at[k], fresh_in.at[h], recv_sem.at[3]).start()

            @pl.when(row != h)
            def _():
                target = fresh_in.at[h]
                put(fresh_out.at[k], target, send_sem.at[3], recv_sem.at[3], hidden=row).start()

    loads[7].wait()
    loads[8].wait()

    @pl.when(h // PAIR == z)
    def _():
        wait_bytes(fresh_in, recv_sem.at[3])
        low = lane < 64
        for g in range(8):
            even = fresh_in[2 * g]
            odd_half = fresh_in[2 * g + 1]
            key = jnp.where(low, even, odd_half)
            value = pltpu.roll(jnp.where(low, odd_half, even), 64, 1)
            key = key * cosine + pltpu.roll(key, 64, 1) * sine
            fresh_rows[0, 0:2, g * 128 : (g + 1) * 128] = key
            fresh_rows[1, 0:2, g * 128 : (g + 1) * 128] = value

    keys[SLOTS:EXTENDED, :] = fresh_rows[0].astype(jnp.bfloat16)
    values[SLOTS:EXTENDED, :] = fresh_rows[1].astype(jnp.bfloat16)

    column = lax.broadcasted_iota(jnp.int32, (2 * N, EXTENDED), 1)
    row_step = lax.rem(lax.broadcasted_iota(jnp.int32, (2 * N, EXTENDED), 0) // GROUP, STEPS)
    here = jnp.where(h // PAIR == z, 1, 0)
    cached = jnp.where(z * SLOTS + column < lengths[0], 1, 0)
    appended = jnp.where(column - SLOTS <= row_step, here, 0)
    valid = jnp.where(column < SLOTS, cached, appended) == 1
    wait_bytes(query_in, recv_sem.at[2])
    span = [slice(g * HEAD_SIZE, (g + 1) * HEAD_SIZE) for g in range(8)]
    scores = []
    for g in range(8):
        q = jnp.concatenate([query_in[2 * g], query_in[2 * g + 1]], axis=0)
        product = lax.dot_general(
            q, keys[:, span[g]], by_rows, preferred_element_type=jnp.float32
        )
        scores.append(product * (HEAD_SIZE**-0.5))
    soft = []
    for g in range(8):
        masked = jnp.where(valid, scores[g], NEGATIVE)
        block_max = jnp.max(masked, axis=1, keepdims=True)
        weights = jnp.where(valid, jnp.exp(masked - block_max), 0.0).astype(jnp.bfloat16)
        block_sum = jnp.sum(weights.astype(jnp.float32), axis=1, keepdims=True)
        soft.append((block_max, block_sum, weights))
    for g in range(8):
        block_max, block_sum, weights = soft[g]
        weighted = jnp.dot(weights, values[:, span[g]], preferred_element_type=jnp.float32)
        filled = block_sum > 0.0
        safe = jnp.where(filled, block_sum, 1.0)
        level = jnp.where(filled, block_max + jnp.log(safe), NEGATIVE)
        block = (weighted / safe).astype(jnp.bfloat16)
        block_out[2 * g] = block[:N]
        block_out[2 * g + 1] = block[N:]
        stat_wide[2 * g * N : 2 * (g + 1) * N, :] = jnp.broadcast_to(level, (2 * N, HEAD_SIZE))
    for half in range(2):
        turned = stat_wide[half * 128 : (half + 1) * 128, :].T
        stat_out[half] = turned[0:1, :]

    def send_block(i, carry):
        to = lax.rem(z + far_first(i), N)
        index = lax.rem(to + N - FIRST_MERGE, N)

        @pl.when(index < SUMS)
        def _():
            stat = stat_out.at[index // (SUMS // 2)]
            block = block_out.at[pl.ds(PAIR * index, PAIR)]
            put(stat, stat_in.at[z], send_sem.at[5], recv_sem.at[5], width=to).start()
            put(block, block_in.at[z], send_sem.at[4], recv_sem.at[4], width=to).start()

        return carry

    lax.fori_loop(0, N - 1, send_block, 0)

    @pl.when(merges_here)
    def _():
        stat = stat_out.at[place // (SUMS // 2)]
        block = block_out.at[pl.ds(PAIR * place, PAIR)]
        pltpu.make_async_copy(stat, stat_in.at[z], recv_sem.at[5]).start()
        pltpu.make_async_copy(block, block_in.at[z], recv_sem.at[4]).start()
        wait_bytes(stat_in, recv_sem.at[5])
        levels = [stat_in[i] for i in range(N)]
        peak = functools.reduce(jnp.maximum, levels)
        factors = [jnp.exp(level - peak) for level in levels]
        denominator = functools.reduce(jnp.add, factors)
        for i in range(N):
            coef[i : i + 1, :] = factors[i] / denominator
        coef[...] = coef[...].T
        first = PAIR * N * lax.rem(place, SUMS // 2)
        mine = coef[pl.ds(pl.multiple_of(first, PAIR * N), PAIR * N), :]
        wait_bytes(block_in, recv_sem.at[4])
        merged = jnp.zeros((PAIR * N, HEAD_SIZE), jnp.float32)
        for i in range(N):
            block = block_in[i].astype(jnp.float32).reshape(PAIR * N, HEAD_SIZE)
            merged = merged + block * mine[:, i : i + 1]
        head_out[...] = merged.astype(jnp.bfloat16).reshape(PAIR, N, HEAD_SIZE)
        broadcast_pair(head_out, head_in, 6, place, True)

    loads[9].wait()
    wait_bytes(head_in, recv_sem.at[6])
    head_wide[...] = head_in[...].astype(jnp.float32).reshape(N * N, HEAD_SIZE)
    attended = jnp.concatenate(
        [head_wide[pl.ds(j, ROWS, stride=GROUP), :].astype(jnp.bfloat16) for j in range(GROUP)],
        axis=1,
    )
    for c in range(4):
        part = jnp.dot(
            attended, w_out[:, c * chunk : (c + 1) * chunk], preferred_element_type=jnp.float32
        )
        wide[pl.ds(2 * c * ROWS, ROWS), :] = part[:, :HEAD_SIZE]
        wide[pl.ds((2 * c + 1) * ROWS, ROWS), :] = part[:, HEAD_SIZE:]
    sent_pairs = SUMS - 1

    wait_bytes(part_in.at[pl.ds(0, sent_pairs)], send_sem.at[0])
    wait_bytes(aux_in.at[pl.ds(0, sent_pairs)], send_sem.at[1])

    @pl.when(jnp.logical_not(sums_here))
    def _():
        wait_bytes(part_in.at[0], send_sem.at[0])
        wait_bytes(aux_in.at[0], send_sem.at[1])

    to_messages(wide, message)

    def send_out(i, carry):
        to = lax.rem(h + far_first(i), N)
        put(message.at[to], out_in.at[h], send_sem.at[7], recv_sem.at[7], hidden=to).start()
        return carry

    lax.fori_loop(0, N - 1, send_out, 0)
    pltpu.make_async_copy(message.at[h], out_in.at[h], recv_sem.at[7]).start()

    wait_bytes(block_in.at[pl.ds(0, sent_pairs)], send_sem.at[4])
    wait_bytes(stat_in.at[pl.ds(0, sent_pairs)], send_sem.at[5])

    @pl.when(jnp.logical_not(merges_here))
    def _():
        wait_bytes(block_in.at[0], send_sem.at[4])
        wait_bytes(stat_in.at[0], send_sem.at[5])

    @pl.when(sums_here)
    def _():
        wait_bytes(query_in.at[pl.ds(0, N - 1)], send_sem.at[2])
        wait_bytes(query_in, send_sem.at[2])
        wait_bytes(fresh_in.at[0], send_sem.at[3])

        @pl.when(h // PAIR != z)
        def _():
            wait_bytes(query_in.at[0], send_sem.at[2])
            wait_bytes(fresh_in.at[0], send_sem.at[3])

    @pl.when(merges_here)
    def _():
        wait_bytes(head_in.at[pl.ds(0, N - 1)], send_sem.at[6])
        wait_bytes(head_in, send_sem.at[6])

        @pl.when(h // PAIR != place)
        def _():
            wait_bytes(head_in.at[0], send_sem.at[6])

    @pl.when(h // PAIR == z)
    def _():
        for _ in range(N - 1):
            wait_bytes(table_out, send_sem.at[8])

    wait_bytes(out_in, recv_sem.at[7])
    total[...] = jnp.sum(out_in[...].astype(jnp.float32), axis=0)
    for c in range(GROUP):
        both_steps = total[pl.ds(c, STEPS, stride=GROUP), :]
        out_ref[0, :, c * HEAD_SIZE : (c + 1) * HEAD_SIZE] = both_steps.astype(jnp.bfloat16)
    wait_bytes(out_in.at[pl.ds(0, N - 1)], send_sem.at[7])


def local(
    tokens,
    norm_gain,
    w_query,
    key_weight,
    value_weight,
    output_weight,
    rotated_key_cache,
    stored_value_cache,
    lengths,
    positions,
):
    vmem = pl.BlockSpec(memory_space=pltpu.VMEM)
    smem = pl.BlockSpec(memory_space=pltpu.SMEM)
    hbm = pl.BlockSpec(memory_space=pltpu.HBM)
    half, full = jnp.bfloat16, jnp.float32
    features = tokens.shape[2]
    columns = w_query.shape[1]
    scratch = [
        pltpu.VMEM(tokens.shape, half),
        pltpu.VMEM(norm_gain.shape, half),
        pltpu.VMEM(w_query.shape, half),
        pltpu.VMEM(key_weight.shape[::-1], half),
        pltpu.VMEM(value_weight.shape[::-1], half),
        pltpu.VMEM(output_weight.shape, half),
        pltpu.VMEM((EXTENDED, 1024), half),
        pltpu.VMEM((EXTENDED, 1024), half),
        pltpu.VMEM((ROWS, features), full),
        pltpu.VMEM((GROUP * ROWS, HEAD_SIZE), full),
        pltpu.VMEM((2, STEPS, HEAD_SIZE), full),
        pltpu.VMEM((PAIR, 2, STEPS, HEAD_SIZE), full),
        pltpu.VMEM((N, N, HEAD_SIZE), half),
        pltpu.VMEM((N, 4, HEAD_SIZE), full),
        pltpu.VMEM((N, PAIR, N, HEAD_SIZE), half),
        pltpu.VMEM((N, PAIR, 4, HEAD_SIZE), full),
        pltpu.VMEM((PAIR, N, HEAD_SIZE), half),
        pltpu.VMEM((PAIR, STEPS, HEAD_SIZE), full),
        pltpu.VMEM((N, N, HEAD_SIZE), half),
        pltpu.VMEM((N, STEPS, HEAD_SIZE), full),
        pltpu.VMEM((2, N, 1024), full),
        pltpu.VMEM((N, N, HEAD_SIZE), half),
        pltpu.VMEM((N * N, HEAD_SIZE), full),
        pltpu.VMEM((2, 1, HEAD_SIZE), full),
        pltpu.VMEM((N, PAIR, N, HEAD_SIZE), half),
        pltpu.VMEM((N, 1, HEAD_SIZE), full),
        pltpu.VMEM((HEAD_SIZE, HEAD_SIZE), full),
        pltpu.VMEM((PAIR, N, HEAD_SIZE), half),
        pltpu.VMEM((N, N, HEAD_SIZE), half),
        pltpu.VMEM((N * N, HEAD_SIZE), full),
        pltpu.VMEM((N, HEAD_SIZE), full),
        pltpu.VMEM((N, N, HEAD_SIZE), half),
        pltpu.SemaphoreType.DMA((11,)),
        pltpu.SemaphoreType.DMA((9,)),
        pltpu.SemaphoreType.DMA((9,)),
    ]
    return pl.pallas_call(
        kernel,
        out_shape=jax.ShapeDtypeStruct((1, STEPS, columns), half),
        in_specs=[smem, smem] + [hbm] * 8,
        out_specs=vmem,
        scratch_shapes=scratch,
        compiler_params=pltpu.CompilerParams(
            collective_id=0, has_side_effects=True, vmem_limit_bytes=60 * 2**20
        ),
        name="decode_block",
    )(
        lengths,
        positions,
        tokens,
        norm_gain,
        w_query,
        key_weight.T,
        value_weight.T,
        output_weight,
        rotated_key_cache,
        stored_value_cache,
    )


def solution(mesh):
    return jax.shard_map(
        local,
        mesh=mesh,
        in_specs=(
            P("batch", None, "width"),
            P("width"),
            P("width", "hidden"),
            P("width", "hidden"),
            P("width", "hidden"),
            P("hidden", "width"),
            P(("batch", "hidden"), "width", None),
            P(("batch", "hidden"), "width", None),
            P(("batch", "hidden")),
            P(("batch", "hidden")),
        ),
        out_specs=P(("batch", "hidden"), None, "width"),
        check_vma=False,
    )
```

```python
import functools
import math

import jax
import jax.numpy as jnp
from jax import lax
from jax.experimental import pallas as pl
from jax.experimental.pallas import tpu as pltpu
from jax.sharding import PartitionSpec as P

MESH = pl.DeviceIdType.MESH
MODEL_DIMENSION = 16384
HEAD_SIZE = 128
N = 16
GROUP = 8
STEPS = 2
ROWS = N * STEPS
SLOTS = 64
SUM_PLACES = 16
MERGE_PLACES = 14
FIRST_SUM, FIRST_SUM_EXTRA = 0, 0
FIRST_MERGE, FIRST_MERGE_EXTRA = 9, 15
EXTENDED = 80
NEGATIVE = -1e30


def wait_bytes(ref, sem):
    pltpu.make_async_copy(ref, ref, sem).wait()


def put(source, target, send, recv, **device):
    return pltpu.make_async_remote_copy(
        source, target, send, recv, device_id=device, device_id_type=MESH
    )


def far_first(i):
    return N // 2 + ((i + 1) // 2) * (2 * lax.rem(i, 2) - 1)


def to_messages(wide, message):
    for row in range(N):
        parts = [wide[pl.ds(STEPS * row + t, GROUP, stride=ROWS), :] for t in range(STEPS)]
        message[row] = jnp.concatenate(parts, axis=0).astype(jnp.bfloat16)


def kernel(
    lengths,
    positions,
    tokens_hbm,
    gain_hbm,
    w_query_hbm,
    key_hbm,
    value_hbm,
    w_out_hbm,
    key_cache_hbm,
    value_cache_hbm,
    out_ref,
    tokens,
    gain_ref,
    w_query,
    w_key,
    w_value,
    w_out,
    keys,
    values,
    flat,
    wide,
    table_out,
    table_in,
    message,
    aux,
    part_in,
    aux_in,
    query_out,
    fresh_out,
    query_in,
    fresh_in,
    fresh_rows,
    block_out,
    stat_wide,
    stat_out,
    block_in,
    stat_in,
    coef,
    turned,
    head_out,
    head_in,
    head_wide,
    total,
    out_in,
    load_sem,
    send_sem,
    recv_sem,
):
    z = lax.axis_index("width")
    h = lax.axis_index("hidden")

    def items(place, first, first_extra, places):
        one = lax.rem(place + N - first, N)
        two = lax.rem(place + N - first_extra, N)
        return (one, one < places), (two + places, two < N - places)

    rows_here = items(z, FIRST_SUM, FIRST_SUM_EXTRA, SUM_PLACES)
    groups_here = items(z, FIRST_MERGE, FIRST_MERGE_EXTRA, MERGE_PLACES)
    extra_row = h >= SUM_PLACES
    row_place = lax.rem(jnp.where(extra_row, h - SUM_PLACES + FIRST_SUM_EXTRA, h + FIRST_SUM), N)
    at_row_place = z == row_place

    chunk = 256
    loads = [
        pltpu.make_async_copy(tokens_hbm, tokens, load_sem.at[0]),
        pltpu.make_async_copy(key_hbm, w_key, load_sem.at[1]),
        pltpu.make_async_copy(value_hbm, w_value, load_sem.at[2]),
    ]
    load_gain = pltpu.make_async_copy(gain_hbm, gain_ref, load_sem.at[10])
    for c in range(4):
        cols = pl.ds(c * chunk, chunk)
        loads.append(
            pltpu.make_async_copy(w_query_hbm.at[:, cols], w_query.at[:, cols], load_sem.at[3 + c])
        )
    loads.append(
        pltpu.make_async_copy(key_cache_hbm.at[0], keys.at[pl.ds(0, SLOTS)], load_sem.at[7])
    )
    loads.append(
        pltpu.make_async_copy(value_cache_hbm.at[0], values.at[pl.ds(0, SLOTS)], load_sem.at[8])
    )
    loads.append(pltpu.make_async_copy(w_out_hbm, w_out, load_sem.at[9]))
    load_gain.start()
    for load in loads:
        load.start()

    barrier = pltpu.get_barrier_semaphore()

    def greet_width(i, carry):
        to = lax.rem(z + far_first(i), N)
        pl.semaphore_signal(barrier, inc=1, device_id={"width": to}, device_id_type=MESH)
        return carry

    def greet_hidden(i, carry):
        to = lax.rem(h + far_first(i), N)
        pl.semaphore_signal(barrier, inc=1, device_id={"hidden": to}, device_id_type=MESH)
        return carry

    lax.fori_loop(0, N - 1, greet_width, 0)
    lax.fori_loop(0, N - 1, greet_hidden, 0)

    lane = lax.broadcasted_iota(jnp.int32, (STEPS, HEAD_SIZE), 1)
    step = lax.broadcasted_iota(jnp.int32, (STEPS, HEAD_SIZE), 0)
    index = jnp.where(lane < 64, lane, lane - 64).astype(jnp.float32)
    frequency = jnp.exp(-math.log(500000.0) * 2.0 * index / HEAD_SIZE)
    angles = (positions[0] + step).astype(jnp.float32) * frequency
    cosine = jnp.cos(angles)
    sine = jnp.where(lane < 64, -jnp.sin(angles), jnp.sin(angles))
    table_out[0] = cosine
    table_out[1] = sine
    fresh_rows[...] = jnp.zeros_like(fresh_rows)
    coef[...] = jnp.zeros_like(coef)

    loads[0].wait()
    load_gain.wait()
    for row in range(N):
        flat[pl.ds(STEPS * row, STEPS), :] = tokens[row].astype(jnp.float32)
    x = flat[...]
    gain = gain_ref[...].astype(jnp.float32).reshape(1, -1)
    squares = jnp.sum(x * x, axis=1, keepdims=True)
    scaled = (x * gain).astype(jnp.bfloat16)
    loads[1].wait()
    loads[2].wait()
    by_rows = (((1,), (1,)), ((), ()))
    new_key = lax.dot_general(scaled, w_key[...], by_rows, preferred_element_type=jnp.float32)
    new_value = lax.dot_general(scaled, w_value[...], by_rows, preferred_element_type=jnp.float32)
    fresh = jnp.concatenate([new_key, new_value], axis=1)
    odd = lax.rem(h, 2) == 1
    fresh = jnp.where(odd, pltpu.roll(fresh, 64, 1), fresh)
    spread = jnp.broadcast_to(squares, (ROWS, HEAD_SIZE))
    for row in range(N):
        aux[row, 0:2, :] = fresh[STEPS * row : STEPS * row + STEPS, :]
        aux[row, 2:4, :] = spread[STEPS * row : STEPS * row + STEPS, :]
    for c in range(4):
        loads[3 + c].wait()
        part = jnp.dot(
            scaled, w_query[:, c * chunk : (c + 1) * chunk], preferred_element_type=jnp.float32
        )
        wide[pl.ds(2 * c * ROWS, ROWS), :] = part[:, :HEAD_SIZE]
        wide[pl.ds((2 * c + 1) * ROWS, ROWS), :] = part[:, HEAD_SIZE:]
    to_messages(wide, message)

    pl.semaphore_wait(barrier, 2 * (N - 1))

    def give_table(item):
        mine, sem = table_in.at[item], 8 + item

        def send_table(i, carry):
            to = lax.rem(h + far_first(i), N)
            put(table_out, mine, send_sem.at[sem], recv_sem.at[sem], hidden=to).start()
            return carry

        lax.fori_loop(0, N - 1, send_table, 0)
        pltpu.make_async_copy(table_out, mine, recv_sem.at[sem]).start()

    pl.when(jnp.logical_and(at_row_place, jnp.logical_not(extra_row)))(lambda: give_table(0))
    pl.when(jnp.logical_and(at_row_place, extra_row))(lambda: give_table(1))

    def send_part(i, carry):
        to = lax.rem(z + far_first(i), N)
        for item, (row, valid) in enumerate(items(to, FIRST_SUM, FIRST_SUM_EXTRA, SUM_PLACES)):

            @pl.when(valid)
            def _():
                send, recv = send_sem.at[0], recv_sem.at[2 * item]
                put(message.at[row], part_in.at[item, z], send, recv, width=to).start()
                send, recv = send_sem.at[1], recv_sem.at[2 * item + 1]
                put(aux.at[row], aux_in.at[item, z], send, recv, width=to).start()

        return carry

    lax.fori_loop(0, N - 1, send_part, 0)
    for item, (row, valid) in enumerate(rows_here):

        @pl.when(valid)
        def _():
            first, second = recv_sem.at[2 * item], recv_sem.at[2 * item + 1]
            pltpu.make_async_copy(message.at[row], part_in.at[item, z], first).start()
            pltpu.make_async_copy(aux.at[row], aux_in.at[item, z], second).start()


    def broadcast(source, target, send, recv, item, far):
        def send_row(i, carry):
            to = lax.rem(z + far_first(i), N) if far else i
            here = jnp.logical_and(to == z, item == h)

            @pl.when(here)
            def _():
                pltpu.make_async_copy(source, target.at[h], recv).start()

            @pl.when(jnp.logical_not(here))
            def _():
                put(source, target.at[h], send, recv, width=to, hidden=item).start()

            return carry

        lax.fori_loop(0, N, send_row, 0)

    def sum_row(item, row):
        first, second = recv_sem.at[2 * item], recv_sem.at[2 * item + 1]
        wait_bytes(table_in.at[item], recv_sem.at[8 + item])
        wait_bytes(aux_in.at[item], second)
        summed = jnp.sum(aux_in[item], axis=0)
        inverse = lax.rsqrt(summed[2:4] / MODEL_DIMENSION + 1e-05)
        fresh_out[item] = summed[0:2] * inverse
        scale, cosines, sines = [
            jnp.concatenate(
                [jnp.broadcast_to(a[t : t + 1], (GROUP, HEAD_SIZE)) for t in range(STEPS)],
                axis=0,
            )
            for a in (inverse, table_in[item, 0], table_in[item, 1])
        ]
        wait_bytes(part_in.at[item], first)
        q = jnp.sum(part_in[item].astype(jnp.float32), axis=0) * scale
        query_out[item] = (q * cosines + pltpu.roll(q, 64, 1) * sines).astype(jnp.bfloat16)
        broadcast(query_out.at[item], query_in, send_sem.at[2], recv_sem.at[4], row, True)

        @pl.when(row == h)
        def _():
            pltpu.make_async_copy(fresh_out.at[item], fresh_in.at[h], recv_sem.at[5]).start()

        @pl.when(row != h)
        def _():
            target = fresh_in.at[h]
            put(fresh_out.at[item], target, send_sem.at[3], recv_sem.at[5], hidden=row).start()

    for item, (row, valid) in enumerate(rows_here):
        pl.when(valid)(functools.partial(sum_row, item, row))

    loads[7].wait()
    loads[8].wait()

    @pl.when(at_row_place)
    def _():
        wait_bytes(fresh_in, recv_sem.at[5])
        low = lane < 64
        for g in range(8):
            even = fresh_in[2 * g]
            odd_half = fresh_in[2 * g + 1]
            key = jnp.where(low, even, odd_half)
            value = pltpu.roll(jnp.where(low, odd_half, even), 64, 1)
            key = key * cosine + pltpu.roll(key, 64, 1) * sine
            fresh_rows[0, 0:2, g * 128 : (g + 1) * 128] = key
            fresh_rows[1, 0:2, g * 128 : (g + 1) * 128] = value

    keys[SLOTS:EXTENDED, :] = fresh_rows[0].astype(jnp.bfloat16)
    values[SLOTS:EXTENDED, :] = fresh_rows[1].astype(jnp.bfloat16)

    column = lax.broadcasted_iota(jnp.int32, (2 * N, EXTENDED), 1)
    row_step = lax.rem(lax.broadcasted_iota(jnp.int32, (2 * N, EXTENDED), 0) // GROUP, STEPS)
    here = jnp.where(at_row_place, 1, 0)
    cached = jnp.where(z * SLOTS + column < lengths[0], 1, 0)
    appended = jnp.where(column - SLOTS <= row_step, here, 0)
    valid = jnp.where(column < SLOTS, cached, appended) == 1
    wait_bytes(query_in, recv_sem.at[4])
    span = [slice(g * HEAD_SIZE, (g + 1) * HEAD_SIZE) for g in range(8)]
    scores = []
    for g in range(8):
        q = jnp.concatenate([query_in[2 * g], query_in[2 * g + 1]], axis=0)
        product = lax.dot_general(
            q, keys[:, span[g]], by_rows, preferred_element_type=jnp.float32
        )
        scores.append(product * (HEAD_SIZE**-0.5))
    soft = []
    for g in range(8):
        masked = jnp.where(valid, scores[g], NEGATIVE)
        block_max = jnp.max(masked, axis=1, keepdims=True)
        weights = jnp.where(valid, jnp.exp(masked - block_max), 0.0).astype(jnp.bfloat16)
        block_sum = jnp.sum(weights.astype(jnp.float32), axis=1, keepdims=True)
        soft.append((block_max, block_sum, weights))
    for g in range(8):
        block_max, block_sum, weights = soft[g]
        weighted = jnp.dot(weights, values[:, span[g]], preferred_element_type=jnp.float32)
        filled = block_sum > 0.0
        safe = jnp.where(filled, block_sum, 1.0)
        level = jnp.where(filled, block_max + jnp.log(safe), NEGATIVE)
        block = (weighted / safe).astype(jnp.bfloat16)
        block_out[2 * g] = block[:N]
        block_out[2 * g + 1] = block[N:]
        stat_wide[2 * g * N : 2 * (g + 1) * N, :] = jnp.broadcast_to(level, (2 * N, HEAD_SIZE))
    for half in range(2):
        levels = stat_wide[half * 128 : (half + 1) * 128, :].T
        stat_out[half] = levels[0:1, :]

    def send_block(i, carry):
        to = lax.rem(z + far_first(i), N)
        for item, (group, valid) in enumerate(items(to, FIRST_MERGE, FIRST_MERGE_EXTRA, MERGE_PLACES)):

            @pl.when(valid)
            def _():
                stat = stat_out.at[group // GROUP]
                send, recv = send_sem.at[5], recv_sem.at[10 + 2 * item]
                put(stat, stat_in.at[item, z], send, recv, width=to).start()
                send, recv = send_sem.at[4], recv_sem.at[11 + 2 * item]
                put(block_out.at[group], block_in.at[item, z], send, recv, width=to).start()

        return carry

    lax.fori_loop(0, N - 1, send_block, 0)
    for item, (group, valid) in enumerate(groups_here):

        @pl.when(valid)
        def _():
            first, second = recv_sem.at[10 + 2 * item], recv_sem.at[11 + 2 * item]
            stat = stat_out.at[group // GROUP]
            pltpu.make_async_copy(stat, stat_in.at[item, z], first).start()
            pltpu.make_async_copy(block_out.at[group], block_in.at[item, z], second).start()


    def merge_group(item, group):
        first, second = recv_sem.at[10 + 2 * item], recv_sem.at[11 + 2 * item]
        wait_bytes(stat_in.at[item], first)
        levels = [stat_in[item, i] for i in range(N)]
        peak = functools.reduce(jnp.maximum, levels)
        factors = [jnp.exp(level - peak) for level in levels]
        denominator = functools.reduce(jnp.add, factors)
        for i in range(N):
            coef[i : i + 1, :] = factors[i] / denominator
        turned[...] = coef[...].T
        mine = turned[pl.ds(pl.multiple_of(lax.rem(group, GROUP) * N, N), N), :]
        wait_bytes(block_in.at[item], second)
        merged = block_in[item, 0].astype(jnp.float32) * mine[:, 0:1]
        for i in range(1, N):
            merged = merged + block_in[item, i].astype(jnp.float32) * mine[:, i : i + 1]
        head_out[item] = merged.astype(jnp.bfloat16)
        broadcast(head_out.at[item], head_in, send_sem.at[6], recv_sem.at[6], group, False)

    for item, (group, valid) in enumerate(groups_here):
        pl.when(valid)(functools.partial(merge_group, item, group))

    loads[9].wait()
    wait_bytes(head_in, recv_sem.at[6])
    head_wide[...] = head_in[...].astype(jnp.float32).reshape(N * N, HEAD_SIZE)
    attended = jnp.concatenate(
        [head_wide[pl.ds(j, ROWS, stride=GROUP), :].astype(jnp.bfloat16) for j in range(GROUP)],
        axis=1,
    )
    for c in range(4):
        part = jnp.dot(
            attended, w_out[:, c * chunk : (c + 1) * chunk], preferred_element_type=jnp.float32
        )
        wide[pl.ds(2 * c * ROWS, ROWS), :] = part[:, :HEAD_SIZE]
        wide[pl.ds((2 * c + 1) * ROWS, ROWS), :] = part[:, HEAD_SIZE:]
    for _, valid in rows_here:

        @pl.when(jnp.logical_not(valid))
        def _():
            wait_bytes(message.at[0], send_sem.at[0])
            wait_bytes(aux.at[0], send_sem.at[1])

    wait_bytes(message.at[pl.ds(0, N - 2)], send_sem.at[0])
    wait_bytes(aux.at[pl.ds(0, N - 2)], send_sem.at[1])
    to_messages(wide, message)

    def send_out(i, carry):
        to = lax.rem(h + far_first(i), N)
        put(message.at[to], out_in.at[h], send_sem.at[7], recv_sem.at[7], hidden=to).start()
        return carry

    lax.fori_loop(0, N - 1, send_out, 0)
    pltpu.make_async_copy(message.at[h], out_in.at[h], recv_sem.at[7]).start()

    wait_bytes(block_out.at[pl.ds(0, N - 2)], send_sem.at[4])
    wait_bytes(stat_in.at[0, pl.ds(0, N - 2)], send_sem.at[5])
    for item in range(2):
        row, has_row = rows_here[item]
        group, has_group = groups_here[item]

        @pl.when(has_row)
        def _():
            wait_bytes(query_in.at[pl.ds(0, N - 1)], send_sem.at[2])

            @pl.when(row != h)
            def _():
                wait_bytes(query_in.at[0], send_sem.at[2])
                wait_bytes(fresh_in.at[0], send_sem.at[3])

        @pl.when(has_group)
        def _():
            wait_bytes(head_in.at[pl.ds(0, N - 1)], send_sem.at[6])

            @pl.when(group != h)
            def _():
                wait_bytes(head_in.at[0], send_sem.at[6])

        @pl.when(jnp.logical_not(has_group))
        def _():
            wait_bytes(block_out.at[0], send_sem.at[4])
            wait_bytes(stat_in.at[0, 0], send_sem.at[5])

        @pl.when(jnp.logical_and(at_row_place, extra_row if item else jnp.logical_not(extra_row)))
        def _():
            for _ in range(N - 1):
                wait_bytes(table_out, send_sem.at[8 + item])

    wait_bytes(out_in, recv_sem.at[7])
    total[...] = jnp.sum(out_in[...].astype(jnp.float32), axis=0)
    for c in range(GROUP):
        both_steps = total[pl.ds(c, STEPS, stride=GROUP), :]
        out_ref[0, :, c * HEAD_SIZE : (c + 1) * HEAD_SIZE] = both_steps.astype(jnp.bfloat16)
    wait_bytes(out_in.at[pl.ds(0, N - 1)], send_sem.at[7])


def local(
    tokens,
    norm_gain,
    w_query,
    key_weight,
    value_weight,
    output_weight,
    rotated_key_cache,
    stored_value_cache,
    lengths,
    positions,
):
    vmem = pl.BlockSpec(memory_space=pltpu.VMEM)
    smem = pl.BlockSpec(memory_space=pltpu.SMEM)
    hbm = pl.BlockSpec(memory_space=pltpu.HBM)
    half, full = jnp.bfloat16, jnp.float32
    features = tokens.shape[2]
    columns = w_query.shape[1]
    scratch = [
        pltpu.VMEM(tokens.shape, half),
        pltpu.VMEM(norm_gain.shape, half),
        pltpu.VMEM(w_query.shape, half),
        pltpu.VMEM(key_weight.shape[::-1], half),
        pltpu.VMEM(value_weight.shape[::-1], half),
        pltpu.VMEM(output_weight.shape, half),
        pltpu.VMEM((EXTENDED, 1024), half),
        pltpu.VMEM((EXTENDED, 1024), half),
        pltpu.VMEM((ROWS, features), full),
        pltpu.VMEM((GROUP * ROWS, HEAD_SIZE), full),
        pltpu.VMEM((2, STEPS, HEAD_SIZE), full),
        pltpu.VMEM((2, 2, STEPS, HEAD_SIZE), full),
        pltpu.VMEM((N, N, HEAD_SIZE), half),
        pltpu.VMEM((N, 4, HEAD_SIZE), full),
        pltpu.VMEM((2, N, N, HEAD_SIZE), half),
        pltpu.VMEM((2, N, 4, HEAD_SIZE), full),
        pltpu.VMEM((2, N, HEAD_SIZE), half),
        pltpu.VMEM((2, STEPS, HEAD_SIZE), full),
        pltpu.VMEM((N, N, HEAD_SIZE), half),
        pltpu.VMEM((N, STEPS, HEAD_SIZE), full),
        pltpu.VMEM((2, N, 1024), full),
        pltpu.VMEM((N, N, HEAD_SIZE), half),
        pltpu.VMEM((N * N, HEAD_SIZE), full),
        pltpu.VMEM((2, 1, HEAD_SIZE), full),
        pltpu.VMEM((2, N, N, HEAD_SIZE), half),
        pltpu.VMEM((2, N, 1, HEAD_SIZE), full),
        pltpu.VMEM((HEAD_SIZE, HEAD_SIZE), full),
        pltpu.VMEM((HEAD_SIZE, HEAD_SIZE), full),
        pltpu.VMEM((2, N, HEAD_SIZE), half),
        pltpu.VMEM((N, N, HEAD_SIZE), half),
        pltpu.VMEM((N * N, HEAD_SIZE), full),
        pltpu.VMEM((N, HEAD_SIZE), full),
        pltpu.VMEM((N, N, HEAD_SIZE), half),
        pltpu.SemaphoreType.DMA((11,)),
        pltpu.SemaphoreType.DMA((10,)),
        pltpu.SemaphoreType.DMA((14,)),
    ]
    return pl.pallas_call(
        kernel,
        out_shape=pltpu.VMEM((1, STEPS, columns), half),
        in_specs=[smem, smem] + [hbm] * 8,
        out_specs=vmem,
        scratch_shapes=scratch,
        compiler_params=pltpu.CompilerParams(
            collective_id=0, has_side_effects=True, vmem_limit_bytes=60 * 2**20
        ),
        name="decode_block",
    )(
        lengths,
        positions,
        tokens,
        norm_gain,
        w_query,
        key_weight.T,
        value_weight.T,
        output_weight,
        rotated_key_cache,
        stored_value_cache,
    )


def solution(mesh):
    return jax.shard_map(
        local,
        mesh=mesh,
        in_specs=(
            P("batch", None, "width"),
            P("width"),
            P("width", "hidden"),
            P("width", "hidden"),
            P("width", "hidden"),
            P("hidden", "width"),
            P(("batch", "hidden"), "width", None),
            P(("batch", "hidden"), "width", None),
            P(("batch", "hidden")),
            P(("batch", "hidden")),
        ),
        out_specs=P(("batch", "hidden"), None, "width"),
        check_vma=False,
    )
```

```python
import functools
import math

import jax
import jax.numpy as jnp
from jax import lax
from jax.experimental import pallas as pl
from jax.experimental.pallas import tpu as pltpu
from jax.sharding import PartitionSpec as P

MESH = pl.DeviceIdType.MESH
MODEL_DIMENSION = 16384
HEAD_SIZE = 128
N = 16
GROUP = 8
STEPS = 2
ROWS = N * STEPS
SLOTS = 64
HALF = N // 2
EXTENDED = 80
NEGATIVE = -1e30


def wait_bytes(ref, sem):
    pltpu.make_async_copy(ref, ref, sem).wait()


def put(source, target, send, recv, **device):
    return pltpu.make_async_remote_copy(
        source, target, send, recv, device_id=device, device_id_type=MESH
    )


def far_first(i):
    return N // 2 + ((i + 1) // 2) * (2 * lax.rem(i, 2) - 1)


def mirror(i):
    return lax.rem(N + 9 - i, N)


def to_messages(wide, message):
    for row in range(N):
        parts = [wide[pl.ds(STEPS * row + t, GROUP, stride=ROWS), :] for t in range(STEPS)]
        message[row] = jnp.concatenate(parts, axis=0).astype(jnp.bfloat16)


def kernel(
    lengths,
    positions,
    tokens_hbm,
    gain_hbm,
    w_query_hbm,
    key_hbm,
    value_hbm,
    w_out_hbm,
    key_cache_hbm,
    value_cache_hbm,
    out_ref,
    tokens,
    gain_ref,
    w_query,
    w_key,
    w_value,
    w_out,
    keys,
    values,
    flat,
    wide,
    table_out,
    table_in,
    message,
    aux,
    part_in,
    aux_in,
    query_out,
    fresh_out,
    query_in,
    fresh_in,
    fresh_rows,
    block_out,
    stat_wide,
    stat_out,
    block_in,
    stat_in,
    coef,
    turned,
    head_out,
    head_in,
    head_wide,
    total,
    out_in,
    load_sem,
    send_sem,
    recv_sem,
):
    z = lax.axis_index("width")
    h = lax.axis_index("hidden")

    mine = mirror(z)
    at_row_place = mine == h

    chunk = 256
    loads = [
        pltpu.make_async_copy(tokens_hbm, tokens, load_sem.at[0]),
        pltpu.make_async_copy(key_hbm, w_key, load_sem.at[1]),
        pltpu.make_async_copy(value_hbm, w_value, load_sem.at[2]),
    ]
    load_gain = pltpu.make_async_copy(gain_hbm, gain_ref, load_sem.at[10])
    for c in range(4):
        cols = pl.ds(c * chunk, chunk)
        loads.append(
            pltpu.make_async_copy(w_query_hbm.at[:, cols], w_query.at[:, cols], load_sem.at[3 + c])
        )
    loads.append(
        pltpu.make_async_copy(key_cache_hbm.at[0], keys.at[pl.ds(0, SLOTS)], load_sem.at[7])
    )
    loads.append(
        pltpu.make_async_copy(value_cache_hbm.at[0], values.at[pl.ds(0, SLOTS)], load_sem.at[8])
    )
    loads.append(pltpu.make_async_copy(w_out_hbm, w_out, load_sem.at[9]))
    load_gain.start()
    for load in loads:
        load.start()

    barrier = pltpu.get_barrier_semaphore()

    def greet_width(i, carry):
        to = lax.rem(z + far_first(i), N)
        pl.semaphore_signal(barrier, inc=1, device_id={"width": to}, device_id_type=MESH)
        return carry

    def greet_hidden(i, carry):
        to = lax.rem(h + far_first(i), N)
        pl.semaphore_signal(barrier, inc=1, device_id={"hidden": to}, device_id_type=MESH)
        return carry

    lax.fori_loop(0, N - 1, greet_width, 0)
    lax.fori_loop(0, N - 1, greet_hidden, 0)

    lane = lax.broadcasted_iota(jnp.int32, (STEPS, HEAD_SIZE), 1)
    step = lax.broadcasted_iota(jnp.int32, (STEPS, HEAD_SIZE), 0)
    index = jnp.where(lane < 64, lane, lane - 64).astype(jnp.float32)
    frequency = jnp.exp(-math.log(500000.0) * 2.0 * index / HEAD_SIZE)
    angles = (positions[0] + step).astype(jnp.float32) * frequency
    cosine = jnp.cos(angles)
    sine = jnp.where(lane < 64, -jnp.sin(angles), jnp.sin(angles))
    table_out[0] = cosine
    table_out[1] = sine
    fresh_rows[...] = jnp.zeros_like(fresh_rows)

    loads[0].wait()
    load_gain.wait()
    for row in range(N):
        flat[pl.ds(STEPS * row, STEPS), :] = tokens[row].astype(jnp.float32)
    x = flat[...]
    gain = gain_ref[...].astype(jnp.float32).reshape(1, -1)
    squares = jnp.sum(x * x, axis=1, keepdims=True)
    scaled = (x * gain).astype(jnp.bfloat16)
    loads[1].wait()
    loads[2].wait()
    by_rows = (((1,), (1,)), ((), ()))
    new_key = lax.dot_general(scaled, w_key[...], by_rows, preferred_element_type=jnp.float32)
    new_value = lax.dot_general(scaled, w_value[...], by_rows, preferred_element_type=jnp.float32)
    fresh = jnp.concatenate([new_key, new_value], axis=1)
    odd = lax.rem(h, 2) == 1
    fresh = jnp.where(odd, pltpu.roll(fresh, 64, 1), fresh)
    spread = jnp.broadcast_to(squares, (ROWS, HEAD_SIZE))
    for row in range(N):
        aux[row, 0:2, :] = fresh[STEPS * row : STEPS * row + STEPS, :]
        aux[row, 2:4, :] = spread[STEPS * row : STEPS * row + STEPS, :]
    for c in range(4):
        loads[3 + c].wait()
        part = jnp.dot(
            scaled, w_query[:, c * chunk : (c + 1) * chunk], preferred_element_type=jnp.float32
        )
        wide[pl.ds(2 * c * ROWS, ROWS), :] = part[:, :HEAD_SIZE]
        wide[pl.ds((2 * c + 1) * ROWS, ROWS), :] = part[:, HEAD_SIZE:]
    to_messages(wide, message)

    pl.semaphore_wait(barrier, 2 * (N - 1))

    @pl.when(at_row_place)
    def _():
        def send_table(i, carry):
            to = lax.rem(h + far_first(i), N)
            put(table_out, table_in, send_sem.at[8], recv_sem.at[8], hidden=to).start()
            return carry

        lax.fori_loop(0, N - 1, send_table, 0)
        pltpu.make_async_copy(table_out, table_in, recv_sem.at[8]).start()

    def send_part(i, carry):
        to = lax.rem(z + far_first(i), N)
        row = mirror(to)
        put(message.at[row], part_in.at[z], send_sem.at[0], recv_sem.at[0], width=to).start()
        put(aux.at[row], aux_in.at[z], send_sem.at[1], recv_sem.at[1], width=to).start()
        return carry

    lax.fori_loop(0, N - 1, send_part, 0)
    pltpu.make_async_copy(message.at[mine], part_in.at[z], recv_sem.at[0]).start()
    pltpu.make_async_copy(aux.at[mine], aux_in.at[z], recv_sem.at[1]).start()

    def broadcast(source, target, send, recv, farthest):
        def send_row(i, carry):
            to = lax.rem(z + far_first(i), N) if farthest else i
            here = jnp.logical_and(to == z, at_row_place)

            @pl.when(here)
            def _():
                pltpu.make_async_copy(source, target.at[h], recv).start()

            @pl.when(jnp.logical_not(here))
            def _():
                put(source, target.at[h], send, recv, width=to, hidden=mine).start()

            return carry

        lax.fori_loop(0, N, send_row, 0)

    wait_bytes(table_in, recv_sem.at[8])
    wait_bytes(aux_in, recv_sem.at[1])
    summed = jnp.sum(aux_in[...], axis=0)
    inverse = lax.rsqrt(summed[2:4] / MODEL_DIMENSION + 1e-05)
    fresh_out[...] = summed[0:2] * inverse
    scale, cosines, sines = [
        jnp.concatenate(
            [jnp.broadcast_to(a[t : t + 1], (GROUP, HEAD_SIZE)) for t in range(STEPS)], axis=0
        )
        for a in (inverse, table_in[0], table_in[1])
    ]
    wait_bytes(part_in, recv_sem.at[0])
    q = jnp.sum(part_in[...].astype(jnp.float32), axis=0) * scale
    query_out[...] = (q * cosines + pltpu.roll(q, 64, 1) * sines).astype(jnp.bfloat16)
    batch = lax.rem(h + 2, N) // HALF
    @pl.when(at_row_place)
    def _():
        pltpu.make_async_copy(fresh_out, fresh_in.at[h], recv_sem.at[4 + batch]).start()

    @pl.when(jnp.logical_not(at_row_place))
    def _():
        recv = recv_sem.at[4 + batch]
        put(fresh_out, fresh_in.at[h], send_sem.at[3], recv, hidden=mine).start()

    broadcast(query_out, query_in, send_sem.at[2], recv_sem.at[2 + batch], True)

    loads[7].wait()
    loads[8].wait()
    low = lane < 64

    def take_fresh(half, heads):
        wait_bytes(fresh_in.at[pl.ds(0, HALF)], recv_sem.at[4 + half])
        for g in heads:
            even = fresh_in[2 * g]
            odd_half = fresh_in[2 * g + 1]
            key = jnp.where(low, even, odd_half)
            value = pltpu.roll(jnp.where(low, odd_half, even), 64, 1)
            key = key * cosine + pltpu.roll(key, 64, 1) * sine
            fresh_rows[0, 0:2, g * 128 : (g + 1) * 128] = key
            fresh_rows[1, 0:2, g * 128 : (g + 1) * 128] = value
            cols = slice(g * HEAD_SIZE, (g + 1) * HEAD_SIZE)
            keys[SLOTS:EXTENDED, cols] = fresh_rows[0, :, cols].astype(jnp.bfloat16)
            values[SLOTS:EXTENDED, cols] = fresh_rows[1, :, cols].astype(jnp.bfloat16)

    keys[SLOTS:EXTENDED, :] = fresh_rows[0].astype(jnp.bfloat16)
    values[SLOTS:EXTENDED, :] = fresh_rows[1].astype(jnp.bfloat16)

    column = lax.broadcasted_iota(jnp.int32, (2 * N, EXTENDED), 1)
    row_step = lax.rem(lax.broadcasted_iota(jnp.int32, (2 * N, EXTENDED), 0) // GROUP, STEPS)
    here = jnp.where(at_row_place, 1, 0)
    cached = jnp.where(z * SLOTS + column < lengths[0], 1, 0)
    appended = jnp.where(column - SLOTS <= row_step, here, 0)
    valid = jnp.where(column < SLOTS, cached, appended) == 1
    span = [slice(g * HEAD_SIZE, (g + 1) * HEAD_SIZE) for g in range(8)]
    coef[...] = jnp.zeros_like(coef)
    for half, heads in enumerate(((7, 0, 1, 2), (3, 4, 5, 6))):
        pl.when(at_row_place)(functools.partial(take_fresh, half, heads))
        wait_bytes(query_in.at[pl.ds(0, HALF)], recv_sem.at[2 + half])
        scores = []
        for g in heads:
            q = jnp.concatenate([query_in[2 * g], query_in[2 * g + 1]], axis=0)
            product = lax.dot_general(
                q, keys[:, span[g]], by_rows, preferred_element_type=jnp.float32
            )
            scores.append(product * (HEAD_SIZE**-0.5))
        soft = []
        for score in scores:
            masked = jnp.where(valid, score, NEGATIVE)
            block_max = jnp.max(masked, axis=1, keepdims=True)
            weights = jnp.where(valid, jnp.exp(masked - block_max), 0.0).astype(jnp.bfloat16)
            block_sum = jnp.sum(weights.astype(jnp.float32), axis=1, keepdims=True)
            soft.append((block_max, block_sum, weights))
        for i, g in enumerate(heads):
            block_max, block_sum, weights = soft[i]
            weighted = jnp.dot(weights, values[:, span[g]], preferred_element_type=jnp.float32)
            filled = block_sum > 0.0
            safe = jnp.where(filled, block_sum, 1.0)
            level = jnp.where(filled, block_max + jnp.log(safe), NEGATIVE)
            block = (weighted / safe).astype(jnp.bfloat16)
            block_out[2 * g] = block[:N]
            block_out[2 * g + 1] = block[N:]
            stat_wide[2 * i * N : 2 * (i + 1) * N, :] = jnp.broadcast_to(level, (2 * N, HEAD_SIZE))
        levels = stat_wide[...].T
        stat_out[half] = levels[0:1, :]

        def send_block(i, carry):
            to = lax.rem(z + far_first(i), N)
            group = mirror(to)

            @pl.when(lax.rem(group + 2, N) // HALF == half)
            def _():
                send, recv = send_sem.at[5], recv_sem.at[10]
                put(stat_out.at[half], stat_in.at[z], send, recv, width=to).start()
                send, recv = send_sem.at[4], recv_sem.at[11]
                put(block_out.at[group], block_in.at[z], send, recv, width=to).start()

            return carry

        lax.fori_loop(0, N - 1, send_block, 0)

        @pl.when(lax.rem(mine + 2, N) // HALF == half)
        def _():
            pltpu.make_async_copy(stat_out.at[half], stat_in.at[z], recv_sem.at[10]).start()
            pltpu.make_async_copy(block_out.at[mine], block_in.at[z], recv_sem.at[11]).start()

    wait_bytes(stat_in, recv_sem.at[10])
    levels = [stat_in[i] for i in range(N)]
    peak = functools.reduce(jnp.maximum, levels)
    factors = [jnp.exp(level - peak) for level in levels]
    denominator = functools.reduce(jnp.add, factors)
    for i in range(N):
        coef[i : i + 1, :] = factors[i] / denominator
    turned[...] = coef[...].T
    shares = turned[pl.ds(pl.multiple_of(lax.rem(mine + 2, GROUP) * N, N), N), :]
    wait_bytes(block_in, recv_sem.at[11])
    merged = block_in[0].astype(jnp.float32) * shares[:, 0:1]
    for i in range(1, N):
        merged = merged + block_in[i].astype(jnp.float32) * shares[:, i : i + 1]
    head_out[...] = merged.astype(jnp.bfloat16)
    broadcast(head_out, head_in, send_sem.at[6], recv_sem.at[6], False)

    loads[9].wait()
    wait_bytes(head_in, recv_sem.at[6])
    head_wide[...] = head_in[...].astype(jnp.float32).reshape(N * N, HEAD_SIZE)
    attended = jnp.concatenate(
        [head_wide[pl.ds(j, ROWS, stride=GROUP), :].astype(jnp.bfloat16) for j in range(GROUP)],
        axis=1,
    )
    for c in range(4):
        part = jnp.dot(
            attended, w_out[:, c * chunk : (c + 1) * chunk], preferred_element_type=jnp.float32
        )
        wide[pl.ds(2 * c * ROWS, ROWS), :] = part[:, :HEAD_SIZE]
        wide[pl.ds((2 * c + 1) * ROWS, ROWS), :] = part[:, HEAD_SIZE:]
    wait_bytes(message.at[pl.ds(0, N - 1)], send_sem.at[0])
    wait_bytes(aux.at[pl.ds(0, N - 1)], send_sem.at[1])
    to_messages(wide, message)

    def send_out(to, carry):
        @pl.when(to != h)
        def _():
            put(message.at[to], out_in.at[h], send_sem.at[7], recv_sem.at[7], hidden=to).start()

        return carry

    lax.fori_loop(0, N, send_out, 0)
    pltpu.make_async_copy(message.at[h], out_in.at[h], recv_sem.at[7]).start()

    wait_bytes(query_in.at[pl.ds(0, N - 1)], send_sem.at[2])
    wait_bytes(block_in.at[pl.ds(0, N - 1)], send_sem.at[4])
    wait_bytes(stat_in.at[pl.ds(0, N - 1)], send_sem.at[5])
    wait_bytes(head_in.at[pl.ds(0, N - 1)], send_sem.at[6])

    @pl.when(jnp.logical_not(at_row_place))
    def _():
        wait_bytes(query_in.at[0], send_sem.at[2])
        wait_bytes(fresh_in.at[0], send_sem.at[3])
        wait_bytes(head_in.at[0], send_sem.at[6])

    @pl.when(at_row_place)
    def _():
        for _ in range(N - 1):
            wait_bytes(table_out, send_sem.at[8])

    wait_bytes(out_in, recv_sem.at[7])
    total[...] = jnp.sum(out_in[...].astype(jnp.float32), axis=0)
    for c in range(GROUP):
        both_steps = total[pl.ds(c, STEPS, stride=GROUP), :]
        out_ref[0, :, c * HEAD_SIZE : (c + 1) * HEAD_SIZE] = both_steps.astype(jnp.bfloat16)
    wait_bytes(out_in.at[pl.ds(0, N - 1)], send_sem.at[7])


def local(
    tokens,
    norm_gain,
    w_query,
    key_weight,
    value_weight,
    output_weight,
    rotated_key_cache,
    stored_value_cache,
    lengths,
    positions,
):
    vmem = pl.BlockSpec(memory_space=pltpu.VMEM)
    smem = pl.BlockSpec(memory_space=pltpu.SMEM)
    hbm = pl.BlockSpec(memory_space=pltpu.HBM)
    half, full = jnp.bfloat16, jnp.float32
    features = tokens.shape[2]
    columns = w_query.shape[1]
    scratch = [
        pltpu.VMEM(tokens.shape, half),
        pltpu.VMEM(norm_gain.shape, half),
        pltpu.VMEM(w_query.shape, half),
        pltpu.VMEM(key_weight.shape[::-1], half),
        pltpu.VMEM(value_weight.shape[::-1], half),
        pltpu.VMEM(output_weight.shape, half),
        pltpu.VMEM((EXTENDED, 1024), half),
        pltpu.VMEM((EXTENDED, 1024), half),
        pltpu.VMEM((ROWS, features), full),
        pltpu.VMEM((GROUP * ROWS, HEAD_SIZE), full),
        pltpu.VMEM((2, STEPS, HEAD_SIZE), full),
        pltpu.VMEM((2, STEPS, HEAD_SIZE), full),
        pltpu.VMEM((N, N, HEAD_SIZE), half),
        pltpu.VMEM((N, 4, HEAD_SIZE), full),
        pltpu.VMEM((N, N, HEAD_SIZE), half),
        pltpu.VMEM((N, 4, HEAD_SIZE), full),
        pltpu.VMEM((N, HEAD_SIZE), half),
        pltpu.VMEM((STEPS, HEAD_SIZE), full),
        pltpu.VMEM((N, N, HEAD_SIZE), half),
        pltpu.VMEM((N, STEPS, HEAD_SIZE), full),
        pltpu.VMEM((2, N, 1024), full),
        pltpu.VMEM((N, N, HEAD_SIZE), half),
        pltpu.VMEM((HALF * N, HEAD_SIZE), full),
        pltpu.VMEM((2, 1, HEAD_SIZE), full),
        pltpu.VMEM((N, N, HEAD_SIZE), half),
        pltpu.VMEM((N, 1, HEAD_SIZE), full),
        pltpu.VMEM((HEAD_SIZE, HEAD_SIZE), full),
        pltpu.VMEM((HEAD_SIZE, HEAD_SIZE), full),
        pltpu.VMEM((N, HEAD_SIZE), half),
        pltpu.VMEM((N, N, HEAD_SIZE), half),
        pltpu.VMEM((N * N, HEAD_SIZE), full),
        pltpu.VMEM((N, HEAD_SIZE), full),
        pltpu.VMEM((N, N, HEAD_SIZE), half),
        pltpu.SemaphoreType.DMA((11,)),
        pltpu.SemaphoreType.DMA((9,)),
        pltpu.SemaphoreType.DMA((12,)),
    ]
    return pl.pallas_call(
        kernel,
        out_shape=pltpu.VMEM((1, STEPS, columns), half),
        in_specs=[smem, smem] + [hbm] * 8,
        out_specs=vmem,
        scratch_shapes=scratch,
        compiler_params=pltpu.CompilerParams(
            collective_id=0, has_side_effects=True, vmem_limit_bytes=60 * 2**20
        ),
        name="decode_block",
    )(
        lengths,
        positions,
        tokens,
        norm_gain,
        w_query,
        key_weight.T,
        value_weight.T,
        output_weight,
        rotated_key_cache,
        stored_value_cache,
    )


def solution(mesh):
    return jax.shard_map(
        local,
        mesh=mesh,
        in_specs=(
            P("batch", None, "width"),
            P("width"),
            P("width", "hidden"),
            P("width", "hidden"),
            P("width", "hidden"),
            P("hidden", "width"),
            P(("batch", "hidden"), "width", None),
            P(("batch", "hidden"), "width", None),
            P(("batch", "hidden")),
            P(("batch", "hidden")),
        ),
        out_specs=P(("batch", "hidden"), None, "width"),
        check_vma=False,
    )
```
